512 devices in a mesh: dp: 128 (over y, z, core), mp: 4 (over x).
Axes of the slice: x: 4, y: 8, z: 8, core: 2. Of those that a mesh axis runs over, the one named last changes fastest.
Arguments:
- train_down: bfloat16 [64, 1024, 7168], P(None, 'dp', 'mp')
- owner: int32 [64], replicated, may hold values from 0 to 63, each once
- trainer_slot: int32 [64], replicated, may hold values from 0 to 63, each once
- expert_act: bfloat16 [4096, 8, 1024], P(('dp', 'mp')), may hold values from -6 to 6
- picks: int32 [4096, 8], P(('dp', 'mp')), may hold values from 0 to 63, all different within a row; in each aligned block of 8 rows (0 to 7, 8 to 15, ...) at most 2 rows name the same one
- route_logits: float32 [4096, 8], P(('dp', 'mp')), may hold values from -6 to 6
- queries: bfloat16 [128, 128, 576], P('dp')
- kv_cache: bfloat16 [128, 2048, 576], P('dp', 'mp')
- lengths: int32 [128], P('dp'), may hold values from 2 to 2048, as said below
Outputs:
- rollout_down: bfloat16 [128, 1024, 3584], P('dp', None, 'mp')
- rollout_scale: float32 [128, 8, 28], P('dp', None, 'mp')
- moe_out: bfloat16 [4096, 7168], P(('dp', 'mp'))
- context: bfloat16 [128, 128, 512], P('dp')
The draws below stay inside these ranges and needn't reach their ends.
Inputs may be any that keep to these rules, and one draw needn't show every extreme that they name: owner gives each expert its own group. trainer_slot gives each expert its own block. `picks`: each row names 8 different experts; within the rows of one device no expert is named more than 2 times, and in some device exactly 2 times. `lengths`: the first sequence has exactly 2048 live positions.
All inputs are finite; a program needn't handle non-finite values.
Results may differ from the reference program's by a relative error of at most 0.017.
Values may be sent and summed in bfloat16 or wider, within the bound.
A program may use at most 64 MiB of HBM per device.

```python
import math
import jax
import jax.numpy as jnp
import numpy as np
from jax import lax

D = 7168
FF = 1024
HEADS = 128
LATENT = 512
ROPE = 64
LEN = 2048
ROWS_DEV = 8
EXPERTS = 64
TOPK = 8
CAP = 2
ROWS = 4096
SEQS = 128
N_DP = 128
N_MP = 4


TARGET_MID = 3000.0


GAP = 2.0


SCALE_SCORE = 192.0 ** (-0.5)


def shared_latents(key):
    return jax.random.normal(key, (SEQS, LEN, LATENT + ROPE), jnp.float32)


def draw_train_down(key, part):
    key = jax.random.fold_in(key, 5)
    row_key, col_key, noise_key = jax.random.split(key, 3)
    reach = 1.15
    noise = jax.random.normal(noise_key, (EXPERTS, FF, D), jnp.float32)
    row_scale = jnp.exp(jax.random.uniform(row_key, (EXPERTS, FF, 1), jnp.float32, -reach, reach))
    col_scale = jnp.exp(jax.random.uniform(col_key, (EXPERTS, 1, D), jnp.float32, -reach, reach))
    return (noise * row_scale * col_scale * FF ** (-0.5)).astype(jnp.bfloat16)


def draw_kv_cache(key, part):
    base = shared_latents(key)
    key = jax.random.fold_in(key, 7)
    noise = jax.random.normal(key, (SEQS, LATENT + ROPE), jnp.float32)
    first = base[:, 0, :]
    energy = jnp.sum(first * first, axis=1, keepdims=True)
    along = jnp.sum(noise * first, axis=1, keepdims=True) / energy
    strength = TARGET_MID / (LATENT + ROPE)
    shift = GAP / (SCALE_SCORE * strength * energy)
    second = first + noise - along * first - shift * first
    base = base.at[:, 0, :].set(first)
    base = base.at[:, 1, :].set(second)
    return base.astype(jnp.bfloat16)


def draw_queries(key, part):
    base = shared_latents(key)
    key = jax.random.fold_in(key, 8)
    fresh = jax.random.normal(key, (SEQS, HEADS, LATENT + ROPE), jnp.float32)
    strength = jnp.array([2000.0, 3000.0, 4000.0], jnp.float32)[jnp.arange(HEADS) % 3] / (LATENT + ROPE)
    aligned = jnp.arange(HEADS) % 8 == 0
    target = strength[None, :, None] * base[:, 0, None, :]
    fresh = jnp.where(aligned[None, :, None], target, fresh)
    return fresh.astype(jnp.bfloat16)


def draw_lengths(key, part):
    key = jax.random.fold_in(key, 9)
    drawn = jax.random.randint(key, (SEQS,), 2, LEN + 1)
    return drawn.at[0].set(LEN).astype(jnp.int32)


def steps_of(rng, shape, cuts, low, largest):
    def one(axis_at, blocks):
        steps = jax.random.uniform(jax.random.fold_in(jax.random.fold_in(rng, 6), axis_at), (blocks,), jnp.float32, low / len(cuts), largest / len(cuts))
        return jnp.repeat(jnp.exp(steps), shape[axis_at] // blocks).reshape((-1,) + (1,) * (len(shape) - axis_at - 1))

    level = one(*cuts[0])
    for cut in cuts[1:]:
        level = level * one(*cut)
    return level


def deal_out(stream_key, own, number, rows, count, top, most, slope):
    sequence = jax.random.permutation(stream_key, count)
    packed, common = portions_of(count, rows * top, most, slope, True), portions_of(count, rows * top, most, slope, False)
    places = jnp.arange(count)

    def named(sizes, turn):
        used = int((sizes > 0).sum())
        fixed = max(1, used // 4)
        passed = fixed + (places - fixed + turn * (used - fixed)) % max(1, count - fixed)
        return jnp.zeros((count,), jnp.int32).at[sequence[jnp.where(places < fixed, places, passed)]].set(jnp.asarray(sizes, jnp.int32))

    sizes = jnp.where(number % 4 == 0, named(packed, number // 4), named(common, number - number // 4 - 1))
    mixed = jax.random.permutation(jax.random.fold_in(own, 3), count)
    giver, sink = mixed[0:count // 2 * 2:2], mixed[1:count // 2 * 2:2]
    margin = jnp.minimum(sizes[giver] - 1, most - sizes[sink]) // 2
    margin = jnp.where((giver == sequence[0]) | (sink == sequence[0]) | (sizes[sink] == 0), 0, jnp.maximum(margin, 0))
    passed = jax.random.randint(jax.random.fold_in(own, 4), (count // 2,), 0, 1 << 20) % (margin + 1)
    sizes = sizes.at[giver].add(-passed).at[sink].add(passed)
    members = jnp.searchsorted(jnp.cumsum(sizes), jnp.arange(rows * top), side="right").astype(jnp.int32)
    table = members.reshape(top, rows).T
    table = table[jax.random.permutation(jax.random.fold_in(own, 1), rows)]
    turn = jax.random.randint(jax.random.fold_in(own, 2), (rows, 1), 0, top)
    return jnp.take_along_axis(table, (jnp.arange(top)[None, :] + turn) % top, axis=1)


def portions_of(count, total, most, slope, full):
    loads = [(1 << 20) // math.isqrt(rank ** slope) + 1 for rank in range(1, count + 1)]
    largest = most if full else min(most, max(-(-total // count), total * loads[0] // sum(loads)))
    least = 1 if total - largest >= count - 1 else 0
    counts, surplus = [largest] + [least] * (count - 1), total - largest - least * (count - 1)
    while surplus > 0:
        free = [i for i in range(1, count) if counts[i] < largest] or [i for i in range(1, count) if counts[i] < most]
        whole, left = sum([loads[i] for i in free]), surplus
        for i in free:
            addition = min(most - counts[i], max(1, left * loads[i] // whole), surplus)
            counts[i] = counts[i] + addition
            surplus = surplus - addition
    return np.array(counts)


def bell_draw(key, shape, scale, most, shards=(), kind=jnp.bfloat16):
    gain = steps_of(key, shape, shards, -0.22, 0.18) if shards else 1.0
    values = jax.random.normal(key, shape, jnp.float32) * scale * gain
    return jnp.minimum(jnp.maximum(values, -most), most).astype(kind)


def setup_inputs(seed: int = 0) -> dict:
    key_list = jax.random.split(jax.random.key(seed), 10)
    train_down = draw_train_down(jax.random.fold_in(key_list[9], 71), 0)
    owner = jax.random.permutation(key_list[1], EXPERTS).astype(jnp.int32)
    trainer_slot = jax.random.permutation(key_list[2], EXPERTS).astype(jnp.int32)
    expert_act = bell_draw(key_list[3], (ROWS, TOPK, FF), 1.0, 6.0, ((0, 512),))
    picks_keys = jax.random.split(jax.random.fold_in(key_list[4], 1), ROWS // ROWS_DEV)
    picks_turns = jax.random.permutation(jax.random.fold_in(key_list[4], 3), ROWS // ROWS_DEV)
    picks = jax.vmap(lambda own, number: deal_out(jax.random.fold_in(key_list[4], 2), own, number, ROWS_DEV, EXPERTS, TOPK, CAP, 2))(picks_keys, picks_turns).reshape((ROWS, TOPK))
    route_logits = bell_draw(key_list[5], (ROWS, TOPK), 1.5, 6.0, ((0, 512),), jnp.float32)
    queries = draw_queries(jax.random.fold_in(key_list[9], 71), 0)
    kv_cache = draw_kv_cache(jax.random.fold_in(key_list[9], 71), 0)
    lengths = draw_lengths(jax.random.fold_in(key_list[9], 71), 0)
    return dict(train_down=train_down, owner=owner, trainer_slot=trainer_slot, expert_act=expert_act, picks=picks, route_logits=route_logits, queries=queries, kv_cache=kv_cache, lengths=lengths)


SCORE_SCALE = 192.0 ** -0.5
ROUTE_SCALE = 2.5
CODE_TOP = 448.0
EPS = 1e-6


def block_code(weight):
    height, across = weight.shape
    blocks = weight.astype(jnp.float32).reshape(height // 128, 128, across // 128, 128)
    scales = (jnp.max(jnp.abs(blocks), axis=(1, 3)) + EPS) / CODE_TOP
    coded = (blocks / scales[:, None, :, None]).astype(jnp.bfloat16)
    usable = (coded.astype(jnp.float32) * scales[:, None, :, None]).astype(jnp.bfloat16)
    return coded.reshape(height, across), scales, usable.reshape(height, across)


def reference(train_down, owner, trainer_slot, expert_act, picks, route_logits, queries, kv_cache, lengths):
    groups = owner.shape[0]
    holder = jnp.argsort(owner).astype(jnp.int32)
    wide = D // (2 * N_MP)

    def sync_group(group):
        expert = holder[group]
        coded, scales, usable = block_code(train_down[trainer_slot[expert]])
        coded = coded.reshape(FF, N_MP, 2, wide).transpose(2, 0, 1, 3).reshape(2, FF, N_MP * wide)
        scales = scales.reshape(FF // 128, N_MP, 2, wide // 128).transpose(2, 0, 1, 3)
        return coded, scales.reshape(2, FF // 128, N_MP * wide // 128)

    coded_all, scale_all = lax.map(sync_group, jnp.arange(groups, dtype=jnp.int32))
    rollout_down = coded_all.reshape(2 * groups, FF, D // 2)
    rollout_scale = scale_all.reshape(2 * groups, FF // 128, D // 256)

    rows = picks.shape[0]
    flat_picks = picks.reshape(-1)
    flat_act = expert_act.reshape(rows * TOPK, FF)
    gates = jax.nn.sigmoid(route_logits.astype(jnp.float32))
    shares = (gates / jnp.sum(gates, axis=1, keepdims=True)).reshape(-1)
    limit = min(N_DP * N_MP * CAP, rows * TOPK)
    row_of_pick = (jnp.arange(rows * TOPK) // TOPK).astype(jnp.int32)

    def add_expert(running, expert):
        order = jnp.argsort((flat_picks != expert).astype(jnp.int32), stable=True)[:limit].astype(jnp.int32)
        live = flat_picks[order] == expert
        _, _, usable = block_code(train_down[trainer_slot[expert]])
        outputs = jnp.dot(flat_act[order], usable, preferred_element_type=jnp.float32).astype(jnp.bfloat16)
        term = outputs.astype(jnp.float32) * jnp.where(live, shares[order], jnp.zeros_like(shares[order]))[:, None]
        return running.at[row_of_pick[order]].add(term), None

    running, _ = lax.scan(add_expert, jnp.zeros((rows, D), jnp.float32), jnp.arange(EXPERTS, dtype=jnp.int32))
    moe_out = (ROUTE_SCALE * running).astype(jnp.bfloat16)

    def attend(items):
        query, cache, length = items
        scores = jnp.einsum("hc,jc->hj", query.astype(jnp.float32), cache.astype(jnp.float32)) * SCORE_SCALE
        live = (jnp.arange(LEN) < length)[None, :]
        masked = jnp.where(live, scores, -1e30)
        peak = jnp.max(masked, axis=1, keepdims=True)
        probs = jnp.where(live, jnp.exp(masked - peak), 0.0)
        total = jnp.sum(probs, axis=1)
        mixed = jnp.einsum("hj,jc->hc", probs.astype(jnp.bfloat16).astype(jnp.float32), cache[:, :LATENT].astype(jnp.float32))
        return (mixed / total[:, None]).astype(jnp.bfloat16)

    context = lax.map(attend, (queries, kv_cache, lengths))
    return rollout_down, rollout_scale, moe_out, context
```

```python
import jax
import jax.numpy as jnp
from jax import lax
from jax.experimental import pallas as pl
from jax.experimental.pallas import tpu as pltpu
from jax.sharding import PartitionSpec as P

LATENT = 512
SCORE_SCALE = 192.0 ** (-0.5)
ROUTE_SCALE = 2.5
CODE_TOP = 448.0
EPS = 1e-06

MESH = pl.DeviceIdType.MESH
F32 = jnp.float32
BF16 = jnp.bfloat16
RING = 8
WIDE = 896
HIDDEN = 1024
BLOCKS = WIDE // 128


def mod8(v):
    return lax.rem(v + 8 * RING, RING)


def kernel(
    src_ref,
    len_ref,
    row_ref,
    coef_ref,
    td_ref,
    act_ref,
    q_ref,
    kv_ref,
    down_ref,
    scale_ref,
    moe_ref,
    ctx_ref,
    wsend,
    wrecv,
    asend,
    arecv,
    bsend,
    afull,
    usable,
    psend,
    precv,
    cbuf,
    xacc,
    xstat,
    moesend,
    moerecv,
    macc,
    scl,
    a_send,
    a_recv,
    b_send,
    b_recv,
    c_send,
    c_recv,
    k_send,
    k_recv,
    w_send,
    w_recv,
    p_send,
    p_recv,
    x_send,
    x_recv,
    m_send,
    m_recv,
):
    d = lax.axis_index("dp")
    m = lax.axis_index("mp")
    line = lax.div(d, 2)
    c = lax.rem(d, 2)
    y = lax.div(line, RING)
    z = lax.rem(line, RING)
    j = c * 4 + m

    def remote(src, dst, send, recv, dt, mt):
        return pltpu.make_async_remote_copy(
            src_ref=src,
            dst_ref=dst,
            send_sem=send,
            recv_sem=recv,
            device_id=(dt, mt),
            device_id_type=MESH,
        )

    def drain(ref, sem):
        pltpu.make_async_copy(ref, ref, sem).wait()

    def mate(k):
        return 2 * line + lax.div(k, 4), lax.rem(k, 4)

    barrier = pltpu.get_barrier_semaphore()

    def greet(i, _):
        pl.semaphore_signal(
            barrier, inc=1, device_id=(lax.rem(d + i, 128), m), device_id_type=MESH
        )
        return 0

    lax.fori_loop(1, 128, greet, 0)
    for dx in range(1, 4):
        for cc in range(2):
            pl.semaphore_signal(
                barrier,
                inc=1,
                device_id=(2 * line + cc, lax.rem(m + dx, 4)),
                device_id_type=MESH,
            )

    acts = act_ref[...].astype(F32).reshape(64, HIDDEN).astype(BF16)
    chooser = (
        (lax.broadcasted_iota(jnp.int32, (128, 64), 0) == row_ref[...]).astype(F32).astype(BF16)
    )
    packed = jnp.dot(chooser, acts, preferred_element_type=F32).astype(BF16)
    asend[...] = packed.reshape(RING, 16, HIDDEN)
    arecv[j] = asend[j]
    cbuf[m] = coef_ref[...]

    pl.semaphore_wait(barrier, 133)

    def a_copy(dj):
        jt = lax.rem(j + dj, RING)
        dt, mt = mate(jt)
        return remote(asend.at[jt], arecv.at[j], a_send.at[dj], a_recv.at[j], dt, mt)

    def a_arrival(dj):
        js = lax.rem(j + dj, RING)
        return remote(asend.at[js], arecv.at[js], a_send.at[dj], a_recv.at[js], d, m)

    for dj in range(1, RING):
        a_copy(dj).start()

    def k_copy(dx):
        mt = lax.rem(m + dx, 4)
        return remote(coef_ref, cbuf.at[m], k_send.at[dx], k_recv.at[m], d, mt)

    for dx in range(1, 4):
        k_copy(dx).start()

    def w_line(t):
        a = lax.div(t, 32)
        b = lax.rem(t, 32)
        b4 = lax.rem(b, 4)
        dy = 2 * b4 + a
        dz = lax.rem(lax.div(b, 4) + 2 * b4, RING)
        return mod8(y + dy) * RING + mod8(z + dz)

    def w_step(t, _):
        lt = w_line(t)
        blk = td_ref[src_ref[lt]]
        for cc in range(2):
            wsend[2 * t + cc] = blk[:, cc * WIDE : (cc + 1) * WIDE]
        for cc in range(2):
            dt = 2 * lt + cc
            remote(wsend.at[2 * t + cc], wrecv.at[d], w_send, w_recv.at[y], dt, m).start()
        return 0

    own = td_ref[src_ref[line]]
    for cc in range(2):
        wsend[cc] = own[:, cc * WIDE : (cc + 1) * WIDE]
    remote(wsend.at[1 - c], wrecv.at[d], w_send, w_recv.at[y], 2 * line + 1 - c, m).start()
    pltpu.make_async_copy(wsend.at[c], wrecv.at[d], w_recv.at[y]).start()
    lax.fori_loop(1, 8, w_step, 0)

    for dj in range(1, RING):
        a_arrival(dj).wait_recv()
    ro = lax.broadcasted_iota(jnp.int32, (128, 128), 0)
    co = lax.broadcasted_iota(jnp.int32, (128, 128), 1)
    want = lax.bitwise_and(lax.shift_right_logical(ro, 1), 7) * 16
    want = want + lax.shift_right_logical(ro, 4) * 2 + lax.bitwise_and(ro, 1)
    perm = (co == want).astype(F32).astype(BF16)
    regrouped = jnp.dot(perm, arecv[...].reshape(128, HIDDEN), preferred_element_type=F32)
    bsend[...] = regrouped.astype(BF16).reshape(RING, 16, HIDDEN)
    r_out = lax.rem(y + z, RING)
    r_in = mod8(j - y - z)

    def b_target(dy):
        yg = mod8(y + dy)
        return yg, yg * RING + mod8(j - y - z - yg)

    def b_copy(dy):
        yg, gl = b_target(dy)
        return remote(
            bsend.at[yg], afull.at[r_out * RING + y], b_send.at[yg], b_recv, 2 * gl + c, m
        )

    for dy in range(RING):
        yg, gl = b_target(dy)

        @pl.when(gl != line)
        def _():
            b_copy(dy).start()

        @pl.when(gl == line)
        def _():
            pltpu.make_async_copy(bsend.at[yg], afull.at[r_out * RING + y], b_recv).start()

    lax.fori_loop(8, 32, w_step, 0)

    mine = afull.at[pl.ds(r_in * RING, RING)]
    drain(mine, b_recv)

    def c_copy(dj):
        dt, mt = mate(lax.rem(j + dj, RING))
        return remote(mine, mine, c_send.at[dj], c_recv.at[r_in], dt, mt)

    for dj in range(1, RING):
        c_copy(dj).start()

    lax.fori_loop(32, 64, w_step, 0)

    query = q_ref[0]
    cache = kv_ref[0]
    scores = (
        lax.dot_general(query, cache, (((1,), (1,)), ((), ())), preferred_element_type=F32)
        * SCORE_SCALE
    )
    span = scores.shape[1]
    live = (m * span + lax.broadcasted_iota(jnp.int32, scores.shape, 1)) < len_ref[0]
    masked = jnp.where(live, scores, -1e30)
    peak = jnp.max(masked, axis=1, keepdims=True)
    probs = jnp.where(live, jnp.exp(masked - peak), 0.0)
    total = jnp.sum(probs, axis=1, keepdims=True)
    mixed = jnp.dot(probs.astype(BF16), cache[:, :LATENT], preferred_element_type=F32)
    lane = lax.broadcasted_iota(jnp.int32, (128, 128), 1)
    xacc[m] = mixed.astype(BF16)
    xstat[m] = jnp.where(lane < 64, peak, total)

    def x_copies(dx):
        mt = lax.rem(m + dx, 4)
        return (
            remote(xacc.at[m], xacc.at[m], x_send.at[0, dx], x_recv.at[0, m], d, mt),
            remote(xstat.at[m], xstat.at[m], x_send.at[1, dx], x_recv.at[1, m], d, mt),
        )

    for dx in range(1, 4):
        for copy in x_copies(dx):
            copy.start()

    def quantize(i, _):
        dy = 2 * lax.rem(i, 4) + lax.div(i, 4)
        ys = mod8(y - dy)
        rows = wrecv.at[pl.ds(16 * ys, 16)]
        drain(rows, w_recv.at[ys])
        w = rows[...].astype(F32).reshape(128, WIDE)
        at = lax.broadcasted_iota(jnp.int32, (1, 128), 1)
        row = jnp.zeros((1, 128), F32)
        for b in range(BLOCKS):
            blk = w[:, b * 128 : (b + 1) * 128]
            top = jnp.max(jnp.max(jnp.abs(blk), axis=0, keepdims=True), axis=1, keepdims=True) + EPS
            scale = top / CODE_TOP
            coded = (blk * (CODE_TOP / top)).astype(BF16)
            down_ref[pl.ds(128 * ys, 128), b * 128 : (b + 1) * 128] = coded
            usable[pl.ds(128 * ys, 128), b * 128 : (b + 1) * 128] = (
                coded.astype(F32) * scale
            ).astype(BF16)
            row = jnp.where(at == b, scale, row)
        scl[pl.ds(ys, 1), :] = row
        return 0

    lax.fori_loop(0, 4, quantize, 0)

    for dx in range(1, 4):
        ms = lax.rem(m + dx, 4)
        remote(xacc.at[ms], xacc.at[ms], x_send.at[0, dx], x_recv.at[0, ms], d, m).wait_recv()
        remote(xstat.at[ms], xstat.at[ms], x_send.at[1, dx], x_recv.at[1, ms], d, m).wait_recv()
    peaks = [xstat[s][:, 0:1] for s in range(4)]
    highest = jnp.maximum(jnp.maximum(peaks[0], peaks[1]), jnp.maximum(peaks[2], peaks[3]))
    weight = jnp.zeros((128, 1), F32)
    blend = jnp.zeros((128, LATENT), F32)
    for s in range(4):
        factor = jnp.exp(peaks[s] - highest)
        weight = weight + xstat[s][:, 64:65] * factor
        blend = blend + xacc[s].astype(F32) * factor
    ctx_ref[...] = (blend / weight).astype(BF16)

    lax.fori_loop(4, 8, quantize, 0)
    scale_ref[...] = scl[:, 0:BLOCKS]

    for dj in range(1, RING):
        js = lax.rem(j + dj, RING)
        r = mod8(js - y - z)
        part = afull.at[pl.ds(r * RING, RING)]
        remote(part, part, c_send.at[dj], c_recv.at[r], d, m).wait_recv()

    def project(i, _):
        r = lax.rem(y + z + i, RING)
        rows = afull[pl.ds(r * RING, RING)].reshape(128, HIDDEN)
        out = jnp.dot(rows, usable[...], preferred_element_type=F32)
        psend[pl.ds(16 * i, 16)] = out.reshape(16, 8, WIDE).astype(BF16)

        def give(b, _):
            yt = mod8(y + lax.div(b, 2))
            cc = lax.rem(b, 2)
            dt = 2 * (yt * RING + mod8(r - yt)) + cc
            src = psend.at[16 * i + 2 * yt + cc]
            dst = precv.at[(r_out * 2 + c) * RING + y]

            @pl.when(dt != d)
            def _():
                remote(src, dst, p_send, p_recv.at[r_out], dt, m).start()

            @pl.when(dt == d)
            def _():
                pltpu.make_async_copy(src, dst, p_recv.at[r_out]).start()

            return 0

        lax.fori_loop(0, 16, give, 0)
        return 0

    lax.fori_loop(0, RING, project, 0)

    for dx in range(1, 4):
        ms = lax.rem(m + dx, 4)
        remote(coef_ref, cbuf.at[ms], k_send.at[dx], k_recv.at[ms], d, m).wait_recv()
    macc[...] = jnp.zeros_like(macc)

    def combine(i, _):
        r = mod8(y + z - i)
        drain(precv.at[pl.ds(16 * r, 16)], p_recv.at[r])
        share = jnp.concatenate([cbuf[s, r] for s in range(4)], axis=0)[:, 0:64]
        high = share.astype(BF16)
        low = (share - high.astype(F32)).astype(BF16)
        both = jnp.concatenate([high, low], axis=0)
        for s in range(2):
            got = precv[pl.ds((2 * r + s) * RING, RING)].astype(F32).reshape(64, WIDE).astype(BF16)
            part = jnp.dot(both, got, preferred_element_type=F32)
            macc[s] += part[0:32] + part[32:64]
        return 0

    lax.fori_loop(0, RING, combine, 0)
    for s in range(4):
        for half in range(2):
            moesend[s, :, half * WIDE : (half + 1) * WIDE] = macc[half, 8 * s : 8 * s + 8].astype(
                BF16
            )

    def m_copy(dx):
        mt = lax.rem(m + dx, 4)
        return remote(moesend.at[mt], moerecv.at[m], m_send.at[dx], m_recv.at[m], d, mt)

    for dx in range(1, 4):
        m_copy(dx).start()
    moerecv[m] = moesend[m]
    for dx in range(1, 4):
        ms = lax.rem(m + dx, 4)
        remote(moesend.at[ms], moerecv.at[ms], m_send.at[dx], m_recv.at[ms], d, m).wait_recv()
    for s in range(4):
        moe_ref[:, s * 2 * WIDE : (s + 1) * 2 * WIDE] = moerecv[s]

    for dj in range(1, RING):
        a_copy(dj).wait_send()
        c_copy(dj).wait_send()
    for dx in range(1, 4):
        k_copy(dx).wait_send()
        m_copy(dx).wait_send()
        for copy in x_copies(dx):
            copy.wait_send()
    for dy in range(RING):
        yg, gl = b_target(dy)

        @pl.when(gl != line)
        def _():
            b_copy(dy).wait_send()

    drain(wsend.at[pl.ds(0, 127)], w_send)
    drain(psend.at[pl.ds(0, 127)], p_send)


def per_device(
    train_down, owner, trainer_slot, expert_act, picks, route_logits, queries, kv_cache, lengths
):
    d = lax.axis_index("dp")
    m = lax.axis_index("mp")
    line = d // 2
    y, z = line // RING, line % RING
    groups = jnp.arange(64, dtype=jnp.int32)
    source = jnp.sum(jnp.where(owner[None, :] == groups[:, None], trainer_slot[None, :], 0), axis=1)
    flat = picks.reshape(64)
    group = jnp.sum(jnp.where(flat[:, None] == groups[None, :], owner[None, :], 0), axis=1)
    earlier = (flat[:, None] == flat[None, :]) & (groups[None, :] < groups[:, None])
    place = jnp.sum(earlier.astype(jnp.int32), axis=1)
    diag = (group // RING + group % RING) % RING
    row = ((diag + y + z) % RING) * 16 + (group // RING) * 2 + place
    column = (group // RING) * 8 + m * 2 + place
    gates = jax.nn.sigmoid(route_logits)
    shares = ROUTE_SCALE * (gates / jnp.sum(gates, axis=1, keepdims=True))
    key = (diag * 128 + column).reshape(8, 8)
    spots = jnp.arange(RING * 128, dtype=jnp.int32).reshape(RING, 1, 1, 128)
    coef = jnp.sum(
        jnp.where(key[None, :, :, None] == spots, shares[None, :, :, None], 0.0), axis=2
    )

    vmem = pl.BlockSpec(memory_space=pltpu.VMEM)
    smem = pl.BlockSpec(memory_space=pltpu.SMEM)
    dma = pltpu.SemaphoreType.DMA
    down, scale, moe, context = pl.pallas_call(
        kernel,
        out_shape=(
            jax.ShapeDtypeStruct((HIDDEN, WIDE), BF16),
            jax.ShapeDtypeStruct((RING, BLOCKS), F32),
            jax.ShapeDtypeStruct((8, 8 * WIDE), BF16),
            jax.ShapeDtypeStruct((128, LATENT), BF16),
        ),
        in_specs=[smem, smem] + [vmem] * 6,
        out_specs=(vmem,) * 4,
        scratch_shapes=[
            pltpu.VMEM((128, 8, WIDE), BF16),
            pltpu.VMEM((128, 8, WIDE), BF16),
            pltpu.VMEM((RING, 16, HIDDEN), BF16),
            pltpu.VMEM((RING, 16, HIDDEN), BF16),
            pltpu.VMEM((RING, 16, HIDDEN), BF16),
            pltpu.VMEM((64, 16, HIDDEN), BF16),
            pltpu.VMEM((HIDDEN, WIDE), BF16),
            pltpu.VMEM((128, 8, WIDE), BF16),
            pltpu.VMEM((128, 8, WIDE), BF16),
            pltpu.VMEM((4, RING, 8, 128), F32),
            pltpu.VMEM((4, 128, LATENT), BF16),
            pltpu.VMEM((4, 128, 128), F32),
            pltpu.VMEM((4, 8, 2 * WIDE), BF16),
            pltpu.VMEM((4, 8, 2 * WIDE), BF16),
            pltpu.VMEM((2, 32, WIDE), F32),
            pltpu.VMEM((RING, 128), F32),
            dma((RING,)),
            dma((RING,)),
            dma((RING,)),
            dma,
            dma((RING,)),
            dma((RING,)),
            dma((4,)),
            dma((4,)),
            dma,
            dma((RING,)),
            dma,
            dma((RING,)),
            dma((2, 4)),
            dma((2, 4)),
            dma((4,)),
            dma((4,)),
        ],
        compiler_params=pltpu.CompilerParams(
            collective_id=0, has_side_effects=True, vmem_limit_bytes=48 * 1024 * 1024
        ),
        cost_estimate=pl.CostEstimate(
            flops=2_200_000_000, bytes_accessed=8_000_000, transcendentals=70_000
        ),
    )(source, lengths, row.reshape(1, 64), coef, train_down, expert_act, queries, kv_cache)
    return (
        down.reshape(1, HIDDEN, WIDE),
        scale.reshape(1, RING, BLOCKS),
        moe,
        context.reshape(1, 128, LATENT),
    )


def solution(mesh):
    placed = (
        P(None, "dp", "mp"),
        P(),
        P(),
        P(("dp", "mp"), None, None),
        P(("dp", "mp"), None),
        P(("dp", "mp"), None),
        P("dp", None, None),
        P("dp", "mp", None),
        P("dp"),
    )
    return jax.shard_map(
        per_device,
        mesh=mesh,
        in_specs=placed,
        out_specs=(
            P("dp", None, "mp"),
            P("dp", None, "mp"),
            P(("dp", "mp"), None),
            P("dp", None, None),
        ),
        check_vma=False,
    )
```

```python
import jax
import jax.numpy as jnp
from jax import lax
from jax.experimental import pallas as pl
from jax.experimental.pallas import tpu as pltpu
from jax.sharding import PartitionSpec as P

LATENT = 512
SCORE_SCALE = 192.0 ** (-0.5)
ROUTE_SCALE = 2.5
CODE_TOP = 448.0
EPS = 1e-06

MESH = pl.DeviceIdType.MESH
F32 = jnp.float32
BF16 = jnp.bfloat16
RING = 8
WIDE = 896
HIDDEN = 1024
BLOCKS = WIDE // 128
LIMIT = 64 * 1024 * 1024
SIDE = (1, 7, 3, 5, 2, 6, 4, 0)


def mod8(v):
    return lax.rem(v + 8 * RING, RING)


def swing(h):
    half = lax.div(h + 1, 2)
    return mod8(jnp.where(lax.rem(h, 2) == 1, half, -half))


def offset(turn, b):
    return swing(lax.rem(turn + b, RING)), swing(b)


def kernel(
    src_ref,
    len_ref,
    owner_ref,
    picks_ref,
    logit_ref,
    td_hbm,
    act_hbm,
    q_hbm,
    kv_hbm,
    down_hbm,
    scale_hbm,
    moe_hbm,
    ctx_hbm,
    down_ref,
    scale_ref,
    moe_ref,
    ctx_ref,
    td_ref,
    act_ref,
    q_ref,
    kv_ref,
    coef_ref,
    wsend,
    wrecv,
    asend,
    arecv,
    bsend,
    afull,
    usable,
    psend,
    precv,
    qsend,
    qrecv,
    kline,
    kout,
    kfin,
    xacc,
    xstat,
    moesend,
    moerecv,
    scl,
    load,
    keep,
    a_send,
    a_recv,
    b_send,
    b_recv,
    c_send,
    c_recv,
    k_send,
    k_recv,
    l_send,
    l_recv,
    w_send,
    w_recv,
    p_send,
    p_recv,
    q_send,
    q_recv,
    x_send,
    x_recv,
    m_send,
    m_recv,
):
    d = lax.axis_index("dp")
    m = lax.axis_index("mp")
    line = lax.div(d, 2)
    c = lax.rem(d, 2)
    y = lax.div(line, RING)
    z = lax.rem(line, RING)
    j = c * 4 + m
    f = jnp.where(c == 0, z, y)
    g = jnp.where(c == 0, y, z)

    def at(ft, gt):
        return jnp.where(c == 0, gt, ft), jnp.where(c == 0, ft, gt)

    def fellow(ft, gt):
        yt, zt = at(ft, gt)
        return 2 * (yt * RING + zt) + c

    def remote(src, dst, send, recv, dt, mt):
        return pltpu.make_async_remote_copy(
            src_ref=src,
            dst_ref=dst,
            send_sem=send,
            recv_sem=recv,
            device_id=(dt, mt),
            device_id_type=MESH,
        )

    def drain(ref, sem):
        pltpu.make_async_copy(ref, ref, sem).wait()

    def mate(k):
        return 2 * line + lax.div(k, 4), lax.rem(k, 4)

    loads = [
        pltpu.make_async_copy(hbm, ref, load.at[n])
        for n, (hbm, ref) in enumerate(
            ((act_hbm, act_ref), (td_hbm, td_ref), (q_hbm, q_ref), (kv_hbm, kv_ref))
        )
    ]
    for copy in loads:
        copy.start()
    results = [
        pltpu.make_async_copy(ref, hbm, keep.at[n])
        for n, (hbm, ref) in enumerate(
            (
                (down_hbm, down_ref),
                (scale_hbm, scale_ref),
                (moe_hbm, moe_ref),
                (ctx_hbm, ctx_ref),
            )
        )
    ]

    barrier = pltpu.get_barrier_semaphore()

    def greet(i, _):
        pl.semaphore_signal(
            barrier, inc=1, device_id=(lax.rem(d + i, 128), m), device_id_type=MESH
        )
        return 0

    lax.fori_loop(1, 128, greet, 0)
    for dx in range(1, 4):
        for cc in range(2):
            pl.semaphore_signal(
                barrier,
                inc=1,
                device_id=(2 * line + cc, lax.rem(m + dx, 4)),
                device_id_type=MESH,
            )

    def iota(shape, axis):
        return lax.broadcasted_iota(jnp.int32, shape, axis)

    def low3(v):
        return lax.bitwise_and(v, 7)

    def high3(v):
        return lax.shift_right_logical(v, 3)

    def column_of(v):
        return jnp.sum(jnp.where(iota((64, 64), 0) == iota((64, 64), 1), v, 0), axis=1, keepdims=True)

    spread = (low3(iota((8, 64), 1)) == iota((8, 64), 0)).astype(F32).astype(BF16)
    held = high3(iota((8, 64), 1)) == iota((8, 64), 0)

    def along(v):
        return jnp.where(held, jnp.dot(v.astype(BF16), spread, preferred_element_type=F32), 0.0)

    flat = jnp.sum(along(picks_ref[...].astype(F32)), axis=0, keepdims=True).astype(jnp.int32)
    owner = column_of(owner_ref[...])
    group = jnp.sum(jnp.where(iota((64, 64), 0) == flat, owner, 0), axis=0, keepdims=True)
    twin = (column_of(flat) == flat) & (iota((64, 64), 0) < iota((64, 64), 1))
    place = jnp.sum(twin.astype(jnp.int32), axis=0, keepdims=True)
    yg, zg = high3(group), low3(group)
    gates = jax.nn.sigmoid(logit_ref[...])
    shares = ROUTE_SCALE * (gates / jnp.sum(gates, axis=1, keepdims=True))
    coarse = shares.astype(BF16).astype(F32)
    coarse, fine = along(coarse).astype(BF16), along(shares - coarse).astype(BF16)
    for core, (gt, ft) in enumerate(((yg, zg), (zg, yg))):
        key = column_of(gt * 128 + ft * 16 + j * 2 + place)
        spots = (iota((64, 1024), 1) == key).astype(F32).astype(BF16)
        coef = jnp.dot(coarse, spots, preferred_element_type=F32)
        coef += jnp.dot(fine, spots, preferred_element_type=F32)
        for n in range(RING):
            coef_ref[core, n] = coef[:, n * 128 : (n + 1) * 128]
    kline[j] = coef_ref[c]

    row = low3(yg + zg + y + z) * 16 + yg * 2 + place
    chooser = (iota((128, 64), 0) == row).astype(F32).astype(BF16)
    loads[0].wait()
    acts = act_ref[...].astype(F32).reshape(64, HIDDEN).astype(BF16)
    packed = jnp.dot(chooser, acts, preferred_element_type=F32).astype(BF16)
    asend[...] = packed.reshape(RING, 16, HIDDEN)
    arecv[j] = asend[j]

    pl.semaphore_wait(barrier, 133)

    def a_copy(dj):
        jt = lax.rem(j + dj, RING)
        dt, mt = mate(jt)
        return remote(asend.at[jt], arecv.at[j], a_send.at[dj], a_recv.at[j], dt, mt)

    def a_arrival(dj):
        js = lax.rem(j + dj, RING)
        return remote(asend.at[js], arecv.at[js], a_send.at[dj], a_recv.at[js], d, m)

    for dj in range(1, RING):
        a_copy(dj).start()

    def k_copy(dj):
        jt = lax.rem(j + dj, RING)
        dt, mt = mate(jt)
        src = coef_ref.at[lax.div(jt, 4)]
        return remote(src, kline.at[j], k_send.at[dj], k_recv.at[j], dt, mt)

    for dj in range(1, RING):
        k_copy(dj).start()

    def w_line(t):
        dy, dz = offset(lax.div(t, RING), lax.rem(t, RING))
        return mod8(y + dy) * RING + mod8(z + dz)

    def w_step(t, _):
        lt = w_line(t)
        blk = td_ref[src_ref[lt]]
        for cc in range(2):
            wsend[2 * t + cc] = blk[:, cc * WIDE : (cc + 1) * WIDE]
        for cc in range(2):
            dt = 2 * lt + cc
            remote(wsend.at[2 * t + cc], wrecv.at[d], w_send, w_recv.at[y], dt, m).start()
        return 0

    loads[1].wait()
    own = td_ref[src_ref[line]]
    for cc in range(2):
        wsend[cc] = own[:, cc * WIDE : (cc + 1) * WIDE]
    remote(wsend.at[1 - c], wrecv.at[d], w_send, w_recv.at[y], 2 * line + 1 - c, m).start()
    pltpu.make_async_copy(wsend.at[c], wrecv.at[d], w_recv.at[y]).start()
    lax.fori_loop(1, 8, w_step, 0)

    for dj in range(1, RING):
        a_arrival(dj).wait_recv()
    ro = lax.broadcasted_iota(jnp.int32, (128, 128), 0)
    co = lax.broadcasted_iota(jnp.int32, (128, 128), 1)
    want = lax.bitwise_and(lax.shift_right_logical(ro, 1), 7) * 16
    want = want + lax.shift_right_logical(ro, 4) * 2 + lax.bitwise_and(ro, 1)
    perm = (co == want).astype(F32).astype(BF16)
    regrouped = jnp.dot(perm, arecv[...].reshape(128, HIDDEN), preferred_element_type=F32)
    bsend[...] = regrouped.astype(BF16).reshape(RING, 16, HIDDEN)
    r_out = lax.rem(y + z, RING)
    r_in = mod8(j - y - z)

    def b_target(dy):
        yg = mod8(y + dy)
        return yg, yg * RING + mod8(j - y - z - yg)

    def b_copy(dy):
        yg, gl = b_target(dy)
        return remote(
            bsend.at[yg], afull.at[r_out * RING + y], b_send.at[yg], b_recv, 2 * gl + c, m
        )

    for dy in range(RING):
        yg, gl = b_target(dy)

        @pl.when(gl != line)
        def _():
            b_copy(dy).start()

        @pl.when(gl == line)
        def _():
            pltpu.make_async_copy(bsend.at[yg], afull.at[r_out * RING + y], b_recv).start()

    for dj in range(1, RING):
        js = lax.rem(j + dj, RING)
        remote(kout, kline.at[js], k_send.at[dj], k_recv.at[js], d, m).wait_recv()
    kout[...] = sum(kline[n] for n in range(RING))
    kfin[g] = kout[g]

    def l_copy(dg):
        gt = mod8(g + dg)
        return remote(kout.at[gt], kfin.at[g], l_send.at[dg], l_recv.at[g], fellow(f, gt), m)

    for dg in range(1, RING):
        l_copy(dg).start()

    lax.fori_loop(8, 14, w_step, 0)

    mine = afull.at[pl.ds(r_in * RING, RING)]
    drain(mine, b_recv)

    def gathered(js):
        return mod8(js - y - z)

    def c_copy(dx, js):
        r = gathered(js)
        part = afull.at[pl.ds(r * RING, RING)]
        dt = 2 * line + (1 - c if dx == 0 else c)
        sem = c_send.at[dx] if js is j else c_send.at[4 + lax.rem(js - m + 4, 4)]
        return remote(part, part, sem, c_recv.at[r], dt, lax.rem(m + dx, 4))

    def along_x(dx):
        return c * 4 + lax.rem(m + dx, 4)

    for dx in range(4):
        c_copy(dx, j).start()

    lax.fori_loop(14, 64, w_step, 0)

    loads[2].wait()
    loads[3].wait()
    query = q_ref[0]
    cache = kv_ref[0]
    scores = (
        lax.dot_general(query, cache, (((0,), (0,)), ((), ())), preferred_element_type=F32)
        * SCORE_SCALE
    )
    span = scores.shape[1]
    live = (m * span + lax.broadcasted_iota(jnp.int32, scores.shape, 1)) < len_ref[0]
    masked = jnp.where(live, scores, -1e30)
    peak = jnp.max(masked, axis=1, keepdims=True)
    probs = jnp.where(live, jnp.exp(masked - peak), 0.0)
    total = jnp.sum(probs, axis=1, keepdims=True)
    mixed = lax.dot_general(
        probs.astype(BF16),
        cache[:LATENT],
        (((1,), (1,)), ((), ())),
        preferred_element_type=F32,
    )
    lane = lax.broadcasted_iota(jnp.int32, (128, 128), 1)
    xacc[m] = mixed.astype(BF16)
    xstat[m] = jnp.where(lane < 64, peak, total)

    def x_copies(dx):
        mt = lax.rem(m + dx, 4)
        return (
            remote(xacc.at[m], xacc.at[m], x_send.at[0, dx], x_recv.at[0, m], d, mt),
            remote(xstat.at[m], xstat.at[m], x_send.at[1, dx], x_recv.at[1, m], d, mt),
        )

    for dx in range(1, 4):
        for copy in x_copies(dx):
            copy.start()

    for dx in range(1, 4):
        js = along_x(dx)
        c_copy(0, js).wait_recv()
        c_copy(0, js).start()

    def quantize(i, _):
        ys = mod8(y - swing(lax.rem(i + RING - 1, RING)))
        rows = wrecv.at[pl.ds(16 * ys, 16)]
        drain(rows, w_recv.at[ys])
        w = rows[...].astype(F32).reshape(128, WIDE)
        at = lax.broadcasted_iota(jnp.int32, (1, 128), 1)
        row = jnp.zeros((1, 128), F32)
        for b in range(BLOCKS):
            blk = w[:, b * 128 : (b + 1) * 128]
            top = jnp.max(jnp.max(jnp.abs(blk), axis=0, keepdims=True), axis=1, keepdims=True) + EPS
            scale = top / CODE_TOP
            coded = (blk * (CODE_TOP / top)).astype(BF16)
            down_ref[pl.ds(128 * ys, 128), b * 128 : (b + 1) * 128] = coded
            usable[pl.ds(128 * ys, 128), b * 128 : (b + 1) * 128] = (
                coded.astype(F32) * scale
            ).astype(BF16)
            row = jnp.where(at == b, scale, row)
        scl[pl.ds(ys, 1), :] = row
        return 0

    lax.fori_loop(0, 4, quantize, 0)

    for dx in range(1, 4):
        ms = lax.rem(m + dx, 4)
        remote(xacc.at[ms], xacc.at[ms], x_send.at[0, dx], x_recv.at[0, ms], d, m).wait_recv()
        remote(xstat.at[ms], xstat.at[ms], x_send.at[1, dx], x_recv.at[1, ms], d, m).wait_recv()
    peaks = [xstat[s][:, 0:1] for s in range(4)]
    highest = jnp.maximum(jnp.maximum(peaks[0], peaks[1]), jnp.maximum(peaks[2], peaks[3]))
    weight = jnp.zeros((128, 1), F32)
    blend = jnp.zeros((128, LATENT), F32)
    for s in range(4):
        factor = jnp.exp(peaks[s] - highest)
        weight = weight + xstat[s][:, 64:65] * factor
        blend = blend + xacc[s].astype(F32) * factor
    ctx_ref[...] = (blend / weight).astype(BF16)
    results[3].start()

    lax.fori_loop(4, 8, quantize, 0)
    results[0].start()
    for b in range(BLOCKS):
        scale_ref[b] = jnp.sum(
            jnp.where(iota((8, 8), 0) == iota((8, 8), 1), scl[:, b : b + 1], 0.0),
            axis=0,
            keepdims=True,
        )
    results[1].start()

    for dx in range(4):
        js = (1 - c) * 4 + lax.rem(m + dx, 4)
        c_copy(0, js).wait_recv()

    def give(part, turn):
        ft = mod8(f + swing(lax.rem(turn + 1, RING)))
        src, dst = psend.at[part * RING + turn], precv.at[part * RING + f]
        return ft, src, dst, p_recv.at[part]

    def send(part, turn):
        ft, src, dst, sem = give(part, turn)
        remote(src, dst, p_send, sem, fellow(ft, g), m).start()

    def project(turn, _):
        ft = mod8(f + swing(lax.rem(turn + 1, RING)))
        parts = []
        for dg in SIDE:
            yt, zt = at(ft, mod8(g + dg))
            parts.append(afull[mod8(yt + zt) * RING + yt])
        rows = jnp.concatenate(parts, axis=0)
        out = jnp.dot(rows, usable[...], preferred_element_type=F32).astype(BF16)
        psend[turn] = out[:64]
        psend[RING + turn] = out[64:]

        @pl.when(turn < RING - 1)
        def _():
            send(0, turn)

        return 0

    lax.fori_loop(0, RING, project, 0)
    for part in range(2):
        _, src, dst, sem = give(part, RING - 1)
        pltpu.make_async_copy(src, dst, sem).start()

    def rest(turn, _):
        send(1, turn)
        return 0

    lax.fori_loop(0, RING - 1, rest, 0)

    for dg in range(1, RING):
        gs = mod8(g + dg)
        remote(kout.at[gs], kfin.at[gs], l_send.at[dg], l_recv.at[gs], d, m).wait_recv()
    mates = high3(iota((64, 128), 0)) == low3(lax.shift_right_logical(iota((64, 128), 1), 1))
    for part in range(2):
        drain(precv.at[pl.ds(part * RING, RING)], p_recv.at[part])
        for b in range(4 * part, 4 * part + 4):
            gt = mod8(g + SIDE[b])
            share = jnp.where(mates, jnp.concatenate([kfin[gt]] * RING, axis=0), 0.0)
            high = share.astype(BF16)
            low = (share - high.astype(F32)).astype(BF16)
            at_b = 16 * (b - 4 * part)
            got = precv[pl.ds(part * RING, RING), pl.ds(at_b, 16), :].reshape(128, WIDE)
            both = jnp.dot(
                jnp.concatenate([high, low], axis=0), got, preferred_element_type=F32
            )
            qsend[b] = (both[:64] + both[64:]).astype(BF16)
            if SIDE[b]:
                remote(
                    qsend.at[b], qrecv.at[b], q_send, q_recv.at[part], fellow(f, gt), m
                ).start()
            else:
                pltpu.make_async_copy(qsend.at[b], qrecv.at[b], q_recv.at[part]).start()

    drain(qrecv.at[pl.ds(0, 4)], q_recv.at[0])
    drain(qrecv.at[pl.ds(4, 4)], q_recv.at[1])
    full = qrecv[0].astype(F32)
    for b in range(1, RING):
        full = full + qrecv[b].astype(F32)
    moesend[...] = full.reshape(RING, 8, WIDE).astype(BF16)

    def m_copy(dj):
        jt = lax.rem(j + dj, RING)
        dt, mt = mate(jt)
        return remote(moesend.at[jt], moerecv.at[j], m_send.at[dj], m_recv.at[j], dt, mt)

    for dj in range(1, RING):
        m_copy(dj).start()
    moerecv[j] = moesend[j]
    for dj in range(1, RING):
        js = lax.rem(j + dj, RING)
        remote(moesend.at[js], moerecv.at[js], m_send.at[dj], m_recv.at[js], d, m).wait_recv()
    for mm in range(4):
        for cc in range(2):
            start = (2 * mm + cc) * WIDE
            moe_ref[:, start : start + WIDE] = moerecv[cc * 4 + mm]
    results[2].start()

    for dj in range(1, RING):
        a_copy(dj).wait_send()
        k_copy(dj).wait_send()
        l_copy(dj).wait_send()
        m_copy(dj).wait_send()
    for dx in range(4):
        c_copy(dx, j).wait_send()
    for dx in range(1, 4):
        c_copy(0, along_x(dx)).wait_send()
        for copy in x_copies(dx):
            copy.wait_send()
    for dy in range(RING):
        yg, gl = b_target(dy)

        @pl.when(gl != line)
        def _():
            b_copy(dy).wait_send()

    drain(wsend.at[pl.ds(0, 127)], w_send)
    drain(psend.at[pl.ds(0, 14)], p_send)
    drain(qsend.at[pl.ds(0, 7)], q_send)
    for copy in results:
        copy.wait()


def hand_out(*refs):
    given, out, held, sem = refs[:4], refs[4:8], refs[8:12], refs[12]
    quarter = HIDDEN // 4
    pieces = [(0, pl.ds(n * quarter, quarter)) for n in range(4)] + [(1, None), (2, None), (3, None)]

    def copy(src, dst, n):
        which, rows = pieces[n]
        if rows is None:
            return pltpu.make_async_copy(src[which], dst[which], sem.at[n])
        return pltpu.make_async_copy(src[which].at[rows], dst[which].at[rows], sem.at[n])

    for n in range(7):
        copy(given, held, n).start()
    for n in range(7):
        copy(given, held, n).wait()
        copy(held, out, n).start()
    for n in range(7):
        copy(held, out, n).wait()


def per_device(
    train_down, owner, trainer_slot, expert_act, picks, route_logits, queries, kv_cache, lengths
):
    groups = jnp.arange(64, dtype=jnp.int32)
    source = jnp.sum(jnp.where(owner[None, :] == groups[:, None], trainer_slot[None, :], 0), axis=1)
    vmem = pl.BlockSpec(memory_space=pltpu.VMEM)
    smem = pl.BlockSpec(memory_space=pltpu.SMEM)
    dma = pltpu.SemaphoreType.DMA
    hbm = pl.BlockSpec(memory_space=pltpu.HBM)
    out_shape = (
        jax.ShapeDtypeStruct((HIDDEN, WIDE), BF16),
        jax.ShapeDtypeStruct((BLOCKS, 1, RING), F32),
        jax.ShapeDtypeStruct((8, 8 * WIDE), BF16),
        jax.ShapeDtypeStruct((128, LATENT), BF16),
    )
    found = pl.pallas_call(
        kernel,
        out_shape=out_shape,
        in_specs=[smem, smem] + [vmem] * 3 + [hbm] * 4,
        out_specs=(pl.BlockSpec(memory_space=pl.ANY),) * 4,
        scratch_shapes=[pltpu.VMEM(out.shape, out.dtype) for out in out_shape]
        + [
            pltpu.VMEM(train_down.shape, BF16),
            pltpu.VMEM(expert_act.shape, BF16),
            pltpu.VMEM((1, 576, 128), BF16),
            pltpu.VMEM((1, 576, 512), BF16),
            pltpu.VMEM((2, RING, 8, 128), F32),
            pltpu.VMEM((128, 8, WIDE), BF16),
            pltpu.VMEM((128, 8, WIDE), BF16),
            pltpu.VMEM((RING, 16, HIDDEN), BF16),
            pltpu.VMEM((RING, 16, HIDDEN), BF16),
            pltpu.VMEM((RING, 16, HIDDEN), BF16),
            pltpu.VMEM((64, 16, HIDDEN), BF16),
            pltpu.VMEM((HIDDEN, WIDE), BF16),
            pltpu.VMEM((16, 64, WIDE), BF16),
            pltpu.VMEM((16, 64, WIDE), BF16),
            pltpu.VMEM((RING, 64, WIDE), BF16),
            pltpu.VMEM((RING, 64, WIDE), BF16),
            pltpu.VMEM((RING, RING, 8, 128), F32),
            pltpu.VMEM((RING, 8, 128), F32),
            pltpu.VMEM((RING, 8, 128), F32),
            pltpu.VMEM((4, 128, LATENT), BF16),
            pltpu.VMEM((4, 128, 128), F32),
            pltpu.VMEM((RING, 8, WIDE), BF16),
            pltpu.VMEM((RING, 8, WIDE), BF16),
            pltpu.VMEM((RING, 128), F32),
            dma((4,)),
            dma((4,)),
            dma((RING,)),
            dma((RING,)),
            dma((RING,)),
            dma,
            dma((RING,)),
            dma((RING,)),
            dma((RING,)),
            dma((RING,)),
            dma((RING,)),
            dma((RING,)),
            dma,
            dma((RING,)),
            dma,
            dma((2,)),
            dma,
            dma((2,)),
            dma((2, 4)),
            dma((2, 4)),
            dma((RING,)),
            dma((RING,)),
        ],
        compiler_params=pltpu.CompilerParams(
            collective_id=0, has_side_effects=True, vmem_limit_bytes=LIMIT
        ),
        cost_estimate=pl.CostEstimate(
            flops=2_200_000_000, bytes_accessed=8_000_000, transcendentals=70_000
        ),
    )(
        source,
        lengths,
        owner.reshape(1, 64),
        picks,
        route_logits,
        train_down,
        expert_act,
        queries.transpose(0, 2, 1),
        kv_cache.transpose(0, 2, 1),
    )
    anywhere = pl.BlockSpec(memory_space=pl.ANY)
    down, scale, moe, context = pl.pallas_call(
        hand_out,
        out_shape=out_shape,
        in_specs=[anywhere] * 4,
        out_specs=(anywhere,) * 4,
        scratch_shapes=[pltpu.VMEM(out.shape, out.dtype) for out in out_shape] + [dma((7,))],
        compiler_params=pltpu.CompilerParams(vmem_limit_bytes=LIMIT),
    )(*found)
    return (
        down.reshape(1, HIDDEN, WIDE),
        scale.transpose(1, 2, 0),
        moe,
        context.reshape(1, 128, LATENT),
    )


def solution(mesh):
    placed = (
        P(None, "dp", "mp"),
        P(),
        P(),
        P(("dp", "mp"), None, None),
        P(("dp", "mp"), None),
        P(("dp", "mp"), None),
        P("dp", None, None),
        P("dp", "mp", None),
        P("dp"),
    )
    return jax.shard_map(
        per_device,
        mesh=mesh,
        in_specs=placed,
        out_specs=(
            P("dp", None, "mp"),
            P("dp", None, "mp"),
            P(("dp", "mp"), None),
            P("dp", None, None),
        ),
        check_vma=False,
    )
```

```python
import jax
import jax.numpy as jnp
from jax import lax
from jax.experimental import pallas as pl
from jax.experimental.pallas import tpu as pltpu
from jax.sharding import PartitionSpec as P

LATENT = 512
SCORE_SCALE = 192.0 ** (-0.5)
ROUTE_SCALE = 2.5
CODE_TOP = 448.0
EPS = 1e-06

MESH = pl.DeviceIdType.MESH
F32 = jnp.float32
BF16 = jnp.bfloat16
RING = 8
WIDE = 896
HIDDEN = 1024
BLOCKS = WIDE // 128
LIMIT = 64 * 1024 * 1024
SIDE = (1, 7, 3, 5, 2, 6, 4, 0)
PARTS = ((0, 4), (4, 7))


def mod8(v):
    return lax.rem(v + 8 * RING, RING)


def swing(h):
    half = lax.div(h + 1, 2)
    return mod8(jnp.where(lax.rem(h, 2) == 1, half, -half))


def offset(turn, b):
    return swing(lax.rem(turn + b, RING)), swing(b)


def kernel(
    src_ref,
    len_ref,
    owner_ref,
    picks_ref,
    logit_ref,
    td_hbm,
    act_hbm,
    q_hbm,
    kv_hbm,
    down_hbm,
    scale_hbm,
    moe_hbm,
    ctx_hbm,
    down_ref,
    scale_ref,
    moe_ref,
    ctx_ref,
    td_ref,
    act_ref,
    q_ref,
    kv_ref,
    coef_ref,
    wsend,
    wrecv,
    asend,
    arecv,
    bsend,
    afull,
    usable,
    psend,
    precv,
    qsend,
    qrecv,
    kline,
    kout,
    kfin,
    xacc,
    xstat,
    moesend,
    moerecv,
    scl,
    load,
    keep,
    a_send,
    a_recv,
    b_send,
    b_recv,
    c_send,
    c_recv,
    k_send,
    k_recv,
    l_send,
    l_recv,
    w_send,
    w_recv,
    p_send,
    p_recv,
    q_send,
    q_recv,
    x_send,
    x_recv,
    m_send,
    m_recv,
):
    d = lax.axis_index("dp")
    m = lax.axis_index("mp")
    line = lax.div(d, 2)
    c = lax.rem(d, 2)
    y = lax.div(line, RING)
    z = lax.rem(line, RING)
    j = c * 4 + m
    f = jnp.where(c == 0, z, y)
    g = jnp.where(c == 0, y, z)

    def at(ft, gt):
        return jnp.where(c == 0, gt, ft), jnp.where(c == 0, ft, gt)

    def fellow(ft, gt):
        yt, zt = at(ft, gt)
        return 2 * (yt * RING + zt) + c

    def remote(src, dst, send, recv, dt, mt):
        return pltpu.make_async_remote_copy(
            src_ref=src,
            dst_ref=dst,
            send_sem=send,
            recv_sem=recv,
            device_id=(dt, mt),
            device_id_type=MESH,
        )

    def drain(ref, sem):
        pltpu.make_async_copy(ref, ref, sem).wait()

    def mate(k):
        return 2 * line + lax.div(k, 4), lax.rem(k, 4)

    loads = [
        pltpu.make_async_copy(hbm, ref, load.at[n])
        for n, (hbm, ref) in enumerate(
            ((act_hbm, act_ref), (td_hbm, td_ref), (q_hbm, q_ref), (kv_hbm, kv_ref))
        )
    ]
    for copy in loads:
        copy.start()
    results = [
        pltpu.make_async_copy(ref, hbm, keep.at[n])
        for n, (hbm, ref) in enumerate(
            (
                (down_hbm, down_ref),
                (scale_hbm, scale_ref),
                (moe_hbm, moe_ref),
                (ctx_hbm, ctx_ref),
            )
        )
    ]

    barrier = pltpu.get_barrier_semaphore()

    def greet(i, _):
        pl.semaphore_signal(
            barrier, inc=1, device_id=(lax.rem(d + i, 128), m), device_id_type=MESH
        )
        return 0

    lax.fori_loop(1, 128, greet, 0)
    for dx in range(1, 4):
        for cc in range(2):
            pl.semaphore_signal(
                barrier,
                inc=1,
                device_id=(2 * line + cc, lax.rem(m + dx, 4)),
                device_id_type=MESH,
            )

    def iota(shape, axis):
        return lax.broadcasted_iota(jnp.int32, shape, axis)

    def low3(v):
        return lax.bitwise_and(v, 7)

    def high3(v):
        return lax.shift_right_logical(v, 3)

    def column_of(v):
        return jnp.sum(jnp.where(iota((64, 64), 0) == iota((64, 64), 1), v, 0), axis=1, keepdims=True)

    spread = (low3(iota((8, 64), 1)) == iota((8, 64), 0)).astype(F32).astype(BF16)
    held = high3(iota((8, 64), 1)) == iota((8, 64), 0)

    def along(v):
        return jnp.where(held, jnp.dot(v.astype(BF16), spread, preferred_element_type=F32), 0.0)

    flat = jnp.sum(along(picks_ref[...].astype(F32)), axis=0, keepdims=True).astype(jnp.int32)
    owner = column_of(owner_ref[...])
    group = jnp.sum(jnp.where(iota((64, 64), 0) == flat, owner, 0), axis=0, keepdims=True)
    twin = (column_of(flat) == flat) & (iota((64, 64), 0) < iota((64, 64), 1))
    place = jnp.sum(twin.astype(jnp.int32), axis=0, keepdims=True)
    yg, zg = high3(group), low3(group)
    gates = jax.nn.sigmoid(logit_ref[...])
    shares = ROUTE_SCALE * (gates / jnp.sum(gates, axis=1, keepdims=True))
    coarse = shares.astype(BF16).astype(F32)
    coarse, fine = along(coarse).astype(BF16), along(shares - coarse).astype(BF16)
    for core, (gt, ft) in enumerate(((yg, zg), (zg, yg))):
        key = column_of(gt * 128 + ft * 16 + j * 2 + place)
        spots = (iota((64, 1024), 1) == key).astype(F32).astype(BF16)
        coef = jnp.dot(coarse, spots, preferred_element_type=F32)
        coef += jnp.dot(fine, spots, preferred_element_type=F32)
        for n in range(RING):
            coef_ref[core, n] = coef[:, n * 128 : (n + 1) * 128]
    kline[j] = coef_ref[c]

    row = low3(yg + zg + y + z) * 16 + yg * 2 + place
    chooser = (iota((128, 64), 0) == row).astype(F32).astype(BF16)
    loads[0].wait()
    acts = act_ref[...].astype(F32).reshape(64, HIDDEN).astype(BF16)
    packed = jnp.dot(chooser, acts, preferred_element_type=F32).astype(BF16)
    asend[...] = packed.reshape(RING, 16, HIDDEN)
    arecv[j] = asend[j]

    pl.semaphore_wait(barrier, 133)

    def a_copy(dj):
        jt = lax.rem(j + dj, RING)
        dt, mt = mate(jt)
        return remote(asend.at[jt], arecv.at[j], a_send.at[dj], a_recv.at[j], dt, mt)

    def a_arrival(dj):
        js = lax.rem(j + dj, RING)
        return remote(asend.at[js], arecv.at[js], a_send.at[dj], a_recv.at[js], d, m)

    for dj in range(1, RING):
        a_copy(dj).start()

    def k_copy(dj):
        jt = lax.rem(j + dj, RING)
        dt, mt = mate(jt)
        src = coef_ref.at[lax.div(jt, 4)]
        return remote(src, kline.at[j], k_send.at[dj], k_recv.at[j], dt, mt)

    for dj in range(1, RING):
        k_copy(dj).start()

    def columns(part):
        first, last = PARTS[part]
        return slice(first * 128, last * 128)

    def w_line(t):
        dy, dz = offset(lax.div(t, RING), lax.rem(t, RING))
        return mod8(y + dy) * RING + mod8(z + dz)

    def w_give(t, cc, part):
        cols = columns(part)
        return wsend.at[2 * t + cc, :, cols], wrecv.at[d, :, cols], w_recv.at[part, y]

    def w_send_line(t, part):
        lt = w_line(t)
        for cc in range(2):
            src, dst, sem = w_give(t, cc, part)
            remote(src, dst, w_send, sem, 2 * lt + cc, m).start()

    def w_step(t, _):
        blk = td_ref[src_ref[w_line(t)]]
        for cc in range(2):
            wsend[2 * t + cc] = blk[:, cc * WIDE : (cc + 1) * WIDE]
        w_send_line(t, 0)
        return 0

    def w_rest(t, _):
        w_send_line(t, 1)
        return 0

    def w_own(part):
        src, dst, sem = w_give(0, 1 - c, part)
        remote(src, dst, w_send, sem, 2 * line + 1 - c, m).start()
        src, dst, sem = w_give(0, c, part)
        pltpu.make_async_copy(src, dst, sem).start()

    loads[1].wait()
    own = td_ref[src_ref[line]]
    for cc in range(2):
        wsend[cc] = own[:, cc * WIDE : (cc + 1) * WIDE]
    w_own(0)
    lax.fori_loop(1, 12, w_step, 0)

    lax.fori_loop(12, 24, w_step, 0)

    for dj in range(1, RING):
        a_arrival(dj).wait_recv()
    ro = lax.broadcasted_iota(jnp.int32, (128, 128), 0)
    co = lax.broadcasted_iota(jnp.int32, (128, 128), 1)
    want = lax.bitwise_and(lax.shift_right_logical(ro, 1), 7) * 16
    want = want + lax.shift_right_logical(ro, 4) * 2 + lax.bitwise_and(ro, 1)
    perm = (co == want).astype(F32).astype(BF16)
    regrouped = jnp.dot(perm, arecv[...].reshape(128, HIDDEN), preferred_element_type=F32)
    bsend[...] = regrouped.astype(BF16).reshape(RING, 16, HIDDEN)
    r_out = lax.rem(y + z, RING)
    r_in = mod8(j - y - z)

    def b_target(dy):
        yg = mod8(y + dy)
        return yg, yg * RING + mod8(j - y - z - yg)

    def b_copy(dy):
        yg, gl = b_target(dy)
        return remote(
            bsend.at[yg], afull.at[r_out * RING + y], b_send.at[yg], b_recv, 2 * gl + c, m
        )

    for dy in range(RING):
        yg, gl = b_target(dy)

        @pl.when(gl != line)
        def _():
            b_copy(dy).start()

        @pl.when(gl == line)
        def _():
            pltpu.make_async_copy(bsend.at[yg], afull.at[r_out * RING + y], b_recv).start()

    for dj in range(1, RING):
        js = lax.rem(j + dj, RING)
        remote(kout, kline.at[js], k_send.at[dj], k_recv.at[js], d, m).wait_recv()
    kout[...] = sum(kline[n] for n in range(RING))
    kfin[g] = kout[g]

    def l_copy(dg):
        gt = mod8(g + dg)
        return remote(kout.at[gt], kfin.at[g], l_send.at[dg], l_recv.at[g], fellow(f, gt), m)

    for dg in range(1, RING):
        l_copy(dg).start()

    lax.fori_loop(24, 48, w_step, 0)

    mine = afull.at[pl.ds(r_in * RING, RING)]
    drain(mine, b_recv)

    def gathered(js):
        return mod8(js - y - z)

    def c_copy(dx, js):
        r = gathered(js)
        part = afull.at[pl.ds(r * RING, RING)]
        dt = 2 * line + (1 - c if dx == 0 else c)
        sem = c_send.at[dx] if js is j else c_send.at[4 + lax.rem(js - m + 4, 4)]
        return remote(part, part, sem, c_recv.at[r], dt, lax.rem(m + dx, 4))

    def along_x(dx):
        return c * 4 + lax.rem(m + dx, 4)

    for dx in range(4):
        c_copy(dx, j).start()

    lax.fori_loop(48, 64, w_step, 0)
    w_own(1)
    lax.fori_loop(1, 32, w_rest, 0)

    for dx in range(1, 4):
        js = along_x(dx)
        c_copy(0, js).wait_recv()
        c_copy(0, js).start()

    lax.fori_loop(32, 64, w_rest, 0)

    loads[2].wait()
    loads[3].wait()
    query = q_ref[0]
    cache = kv_ref[0]
    scores = (
        lax.dot_general(query, cache, (((0,), (0,)), ((), ())), preferred_element_type=F32)
        * SCORE_SCALE
    )
    span = scores.shape[1]
    live = (m * span + lax.broadcasted_iota(jnp.int32, scores.shape, 1)) < len_ref[0]
    masked = jnp.where(live, scores, -1e30)
    peak = jnp.max(masked, axis=1, keepdims=True)
    probs = jnp.where(live, jnp.exp(masked - peak), 0.0)
    total = jnp.sum(probs, axis=1, keepdims=True)
    mixed = lax.dot_general(
        probs.astype(BF16),
        cache[:LATENT],
        (((1,), (1,)), ((), ())),
        preferred_element_type=F32,
    )
    lane = lax.broadcasted_iota(jnp.int32, (128, 128), 1)
    xacc[m] = mixed.astype(BF16)
    xstat[m] = jnp.where(lane < 64, peak, total)

    def x_copies(dx):
        mt = lax.rem(m + dx, 4)
        return (
            remote(xacc.at[m], xacc.at[m], x_send.at[0, dx], x_recv.at[0, m], d, mt),
            remote(xstat.at[m], xstat.at[m], x_send.at[1, dx], x_recv.at[1, m], d, mt),
        )

    for dx in range(1, 4):
        for copy in x_copies(dx):
            copy.start()

    def quantize(part, i):
        ys = mod8(y - swing(lax.rem(i + RING - 1, RING)))
        rows = wrecv.at[pl.ds(16 * ys, 16), :, columns(part)]
        drain(rows, w_recv.at[part, ys])
        first, last = PARTS[part]
        w = rows[...].astype(F32).reshape(128, (last - first) * 128)
        row = jnp.zeros((1, 128), F32)
        for b in range(first, last):
            blk = w[:, (b - first) * 128 : (b - first + 1) * 128]
            top = jnp.max(jnp.max(jnp.abs(blk), axis=0, keepdims=True), axis=1, keepdims=True) + EPS
            scale = top / CODE_TOP
            coded = (blk * (CODE_TOP / top)).astype(BF16)
            down_ref[pl.ds(128 * ys, 128), b * 128 : (b + 1) * 128] = coded
            usable[pl.ds(128 * ys, 128), b * 128 : (b + 1) * 128] = (
                coded.astype(F32) * scale
            ).astype(BF16)
            row = jnp.where(iota((1, 128), 1) == b, scale, row)
        scl[part, pl.ds(ys, 1), :] = row

    def requantize(part):
        def step(i, _):
            quantize(part, i)
            return 0

        lax.fori_loop(0, RING, step, 0)

    requantize(0)

    for dx in range(4):
        js = (1 - c) * 4 + lax.rem(m + dx, 4)
        c_copy(0, js).wait_recv()

    def give(part, turn):
        ft = mod8(f + swing(lax.rem(turn + 1, RING)))
        cols = columns(part)
        return ft, psend.at[turn, :, cols], precv.at[f, :, cols], p_recv.at[part]

    def project(part):
        def step(turn, _):
            ft, src, dst, sem = give(part, turn)
            parts = []
            for dg in SIDE:
                yt, zt = at(ft, mod8(g + dg))
                parts.append(afull[mod8(yt + zt) * RING + yt])
            rows = jnp.concatenate(parts, axis=0)
            weights = usable[:, columns(part)]
            src[...] = jnp.dot(rows, weights, preferred_element_type=F32).astype(BF16)

            @pl.when(turn < RING - 1)
            def _():
                remote(src, dst, p_send, sem, fellow(ft, g), m).start()

            @pl.when(turn == RING - 1)
            def _():
                pltpu.make_async_copy(src, dst, sem).start()

            return 0

        lax.fori_loop(0, RING, step, 0)

    project(0)
    requantize(1)
    results[0].start()
    for b in range(BLOCKS):
        scale_ref[b] = jnp.sum(
            jnp.where(iota((8, 8), 0) == iota((8, 8), 1), scl[b // 4, :, b : b + 1], 0.0),
            axis=0,
            keepdims=True,
        )
    results[1].start()

    project(1)

    for dx in range(1, 4):
        ms = lax.rem(m + dx, 4)
        remote(xacc.at[ms], xacc.at[ms], x_send.at[0, dx], x_recv.at[0, ms], d, m).wait_recv()
        remote(xstat.at[ms], xstat.at[ms], x_send.at[1, dx], x_recv.at[1, ms], d, m).wait_recv()
    peaks = [xstat[s][:, 0:1] for s in range(4)]
    highest = jnp.maximum(jnp.maximum(peaks[0], peaks[1]), jnp.maximum(peaks[2], peaks[3]))
    weight = jnp.zeros((128, 1), F32)
    blend = jnp.zeros((128, LATENT), F32)
    for s in range(4):
        factor = jnp.exp(peaks[s] - highest)
        weight = weight + xstat[s][:, 64:65] * factor
        blend = blend + xacc[s].astype(F32) * factor
    ctx_ref[...] = (blend / weight).astype(BF16)
    results[3].start()

    for dg in range(1, RING):
        gs = mod8(g + dg)
        remote(kout.at[gs], kfin.at[gs], l_send.at[dg], l_recv.at[gs], d, m).wait_recv()
    mates = high3(iota((64, 128), 0)) == low3(lax.shift_right_logical(iota((64, 128), 1), 1))
    for part in range(2):
        cols = columns(part)
        drain(precv.at[:, :, cols], p_recv.at[part])
        for b in range(RING):
            gt = mod8(g + SIDE[b])
            share = jnp.where(mates, jnp.concatenate([kfin[gt]] * RING, axis=0), 0.0)
            high = share.astype(BF16)
            low = (share - high.astype(F32)).astype(BF16)
            got = precv[:, 16 * b : 16 * b + 16, cols].reshape(128, cols.stop - cols.start)
            both = jnp.dot(jnp.concatenate([high, low], axis=0), got, preferred_element_type=F32)
            src, dst = qsend.at[b, :, cols], qrecv.at[b, :, cols]
            src[...] = (both[:64] + both[64:]).astype(BF16)
            if SIDE[b]:
                remote(src, dst, q_send, q_recv.at[part], fellow(f, gt), m).start()
            else:
                pltpu.make_async_copy(src, dst, q_recv.at[part]).start()

    for part in range(2):
        cols = columns(part)
        drain(qrecv.at[:, :, cols], q_recv.at[part])
        full = qrecv[0, :, cols].astype(F32)
        for b in range(1, RING):
            full = full + qrecv[b, :, cols].astype(F32)
        moesend[:, :, cols] = full.reshape(RING, 8, cols.stop - cols.start).astype(BF16)

    def m_copy(dj):
        jt = lax.rem(j + dj, RING)
        dt, mt = mate(jt)
        return remote(moesend.at[jt], moerecv.at[j], m_send.at[dj], m_recv.at[j], dt, mt)

    for dj in range(1, RING):
        m_copy(dj).start()
    moerecv[j] = moesend[j]
    for dj in range(1, RING):
        js = lax.rem(j + dj, RING)
        remote(moesend.at[js], moerecv.at[js], m_send.at[dj], m_recv.at[js], d, m).wait_recv()
    for mm in range(4):
        for cc in range(2):
            start = (2 * mm + cc) * WIDE
            moe_ref[:, start : start + WIDE] = moerecv[cc * 4 + mm]
    results[2].start()

    for dj in range(1, RING):
        a_copy(dj).wait_send()
        k_copy(dj).wait_send()
        l_copy(dj).wait_send()
        m_copy(dj).wait_send()
    for dx in range(4):
        c_copy(dx, j).wait_send()
    for dx in range(1, 4):
        c_copy(0, along_x(dx)).wait_send()
        for copy in x_copies(dx):
            copy.wait_send()
    for dy in range(RING):
        yg, gl = b_target(dy)

        @pl.when(gl != line)
        def _():
            b_copy(dy).wait_send()

    drain(wsend.at[pl.ds(0, 127)], w_send)
    drain(psend.at[pl.ds(0, 7)], p_send)
    drain(qsend.at[pl.ds(0, 7)], q_send)
    for copy in results:
        copy.wait()


def hand_out(*refs):
    given, out, held, sem = refs[:4], refs[4:8], refs[8:12], refs[12]
    quarter = HIDDEN // 4
    pieces = [(0, pl.ds(n * quarter, quarter)) for n in range(4)] + [(1, None), (2, None), (3, None)]

    def copy(src, dst, n):
        which, rows = pieces[n]
        if rows is None:
            return pltpu.make_async_copy(src[which], dst[which], sem.at[n])
        return pltpu.make_async_copy(src[which].at[rows], dst[which].at[rows], sem.at[n])

    for n in range(7):
        copy(given, held, n).start()
    for n in range(7):
        copy(given, held, n).wait()
        copy(held, out, n).start()
    for n in range(7):
        copy(held, out, n).wait()


def per_device(
    train_down, owner, trainer_slot, expert_act, picks, route_logits, queries, kv_cache, lengths
):
    groups = jnp.arange(64, dtype=jnp.int32)
    source = jnp.sum(jnp.where(owner[None, :] == groups[:, None], trainer_slot[None, :], 0), axis=1)
    vmem = pl.BlockSpec(memory_space=pltpu.VMEM)
    smem = pl.BlockSpec(memory_space=pltpu.SMEM)
    dma = pltpu.SemaphoreType.DMA
    hbm = pl.BlockSpec(memory_space=pltpu.HBM)
    out_shape = (
        jax.ShapeDtypeStruct((HIDDEN, WIDE), BF16),
        jax.ShapeDtypeStruct((BLOCKS, 1, RING), F32),
        jax.ShapeDtypeStruct((8, 8 * WIDE), BF16),
        jax.ShapeDtypeStruct((128, LATENT), BF16),
    )
    found = pl.pallas_call(
        kernel,
        out_shape=out_shape,
        in_specs=[smem, smem] + [vmem] * 3 + [hbm] * 4,
        out_specs=(pl.BlockSpec(memory_space=pl.ANY),) * 4,
        scratch_shapes=[pltpu.VMEM(out.shape, out.dtype) for out in out_shape]
        + [
            pltpu.VMEM(train_down.shape, BF16),
            pltpu.VMEM(expert_act.shape, BF16),
            pltpu.VMEM((1, 576, 128), BF16),
            pltpu.VMEM((1, 576, 512), BF16),
            pltpu.VMEM((2, RING, 8, 128), F32),
            pltpu.VMEM((128, 8, WIDE), BF16),
            pltpu.VMEM((128, 8, WIDE), BF16),
            pltpu.VMEM((RING, 16, HIDDEN), BF16),
            pltpu.VMEM((RING, 16, HIDDEN), BF16),
            pltpu.VMEM((RING, 16, HIDDEN), BF16),
            pltpu.VMEM((64, 16, HIDDEN), BF16),
            pltpu.VMEM((HIDDEN, WIDE), BF16),
            pltpu.VMEM((RING, 128, WIDE), BF16),
            pltpu.VMEM((RING, 128, WIDE), BF16),
            pltpu.VMEM((RING, 64, WIDE), BF16),
            pltpu.VMEM((RING, 64, WIDE), BF16),
            pltpu.VMEM((RING, RING, 8, 128), F32),
            pltpu.VMEM((RING, 8, 128), F32),
            pltpu.VMEM((RING, 8, 128), F32),
            pltpu.VMEM((4, 128, LATENT), BF16),
            pltpu.VMEM((4, 128, 128), F32),
            pltpu.VMEM((RING, 8, WIDE), BF16),
            pltpu.VMEM((RING, 8, WIDE), BF16),
            pltpu.VMEM((2, RING, 128), F32),
            dma((4,)),
            dma((4,)),
            dma((RING,)),
            dma((RING,)),
            dma((RING,)),
            dma,
            dma((RING,)),
            dma((RING,)),
            dma((RING,)),
            dma((RING,)),
            dma((RING,)),
            dma((RING,)),
            dma,
            dma((2, RING)),
            dma,
            dma((2,)),
            dma,
            dma((2,)),
            dma((2, 4)),
            dma((2, 4)),
            dma((RING,)),
            dma((RING,)),
        ],
        compiler_params=pltpu.CompilerParams(
            collective_id=0, has_side_effects=True, vmem_limit_bytes=LIMIT
        ),
        cost_estimate=pl.CostEstimate(
            flops=2_200_000_000, bytes_accessed=8_000_000, transcendentals=70_000
        ),
    )(
        source,
        lengths,
        owner.reshape(1, 64),
        picks,
        route_logits,
        train_down,
        expert_act,
        queries.transpose(0, 2, 1),
        kv_cache.transpose(0, 2, 1),
    )
    anywhere = pl.BlockSpec(memory_space=pl.ANY)
    down, scale, moe, context = pl.pallas_call(
        hand_out,
        out_shape=out_shape,
        in_specs=[anywhere] * 4,
        out_specs=(anywhere,) * 4,
        scratch_shapes=[pltpu.VMEM(out.shape, out.dtype) for out in out_shape] + [dma((7,))],
        compiler_params=pltpu.CompilerParams(vmem_limit_bytes=LIMIT),
    )(*found)
    return (
        down.reshape(1, HIDDEN, WIDE),
        scale.transpose(1, 2, 0),
        moe,
        context.reshape(1, 128, LATENT),
    )


def solution(mesh):
    placed = (
        P(None, "dp", "mp"),
        P(),
        P(),
        P(("dp", "mp"), None, None),
        P(("dp", "mp"), None),
        P(("dp", "mp"), None),
        P("dp", None, None),
        P("dp", "mp", None),
        P("dp"),
    )
    return jax.shard_map(
        per_device,
        mesh=mesh,
        in_specs=placed,
        out_specs=(
            P("dp", None, "mp"),
            P("dp", None, "mp"),
            P(("dp", "mp"), None),
            P("dp", None, None),
        ),
        check_vma=False,
    )
```

```python
import jax
import jax.numpy as jnp
from jax import lax
from jax.experimental import pallas as pl
from jax.experimental.pallas import tpu as pltpu
from jax.sharding import PartitionSpec as P

LATENT = 512
SCORE_SCALE = 192.0 ** (-0.5)
ROUTE_SCALE = 2.5
CODE_TOP = 448.0
EPS = 1e-06

MESH = pl.DeviceIdType.MESH
F32 = jnp.float32
BF16 = jnp.bfloat16
RING = 8
WIDE = 896
HIDDEN = 1024
BLOCKS = WIDE // 128
LIMIT = 64 * 1024 * 1024
SIDE = (1, 7, 3, 5, 2, 6, 4, 0)
PARTS = ((0, 5), (5, 7))


def mod8(v):
    return lax.rem(v + 8 * RING, RING)


def swing(h):
    half = lax.div(h + 1, 2)
    return mod8(jnp.where(lax.rem(h, 2) == 1, half, -half))


def offset(turn, b):
    return swing(lax.rem(turn + b, RING)), swing(b)


def kernel(
    src_ref,
    len_ref,
    owner_ref,
    picks_ref,
    logit_ref,
    td_hbm,
    act_hbm,
    q_hbm,
    kv_hbm,
    down_hbm,
    scale_hbm,
    moe_hbm,
    ctx_hbm,
    down_ref,
    scale_ref,
    moe_ref,
    ctx_ref,
    td_ref,
    act_ref,
    q_ref,
    kv_ref,
    coef_ref,
    wsend,
    wrecv,
    asend,
    arecv,
    bsend,
    afull,
    usable,
    psend,
    precv,
    qsend,
    qrecv,
    kline,
    kout,
    kfin,
    xacc,
    xstat,
    moesend,
    moerecv,
    scl,
    load,
    keep,
    a_send,
    a_recv,
    b_send,
    b_recv,
    c_send,
    c_recv,
    k_send,
    k_recv,
    l_send,
    l_recv,
    w_send,
    w_recv,
    p_send,
    p_recv,
    q_send,
    q_recv,
    x_send,
    x_recv,
    m_send,
    m_recv,
):
    d = lax.axis_index("dp")
    m = lax.axis_index("mp")
    line = lax.div(d, 2)
    c = lax.rem(d, 2)
    y = lax.div(line, RING)
    z = lax.rem(line, RING)
    j = c * 4 + m
    f = jnp.where(c == 0, z, y)
    g = jnp.where(c == 0, y, z)

    def at(ft, gt):
        return jnp.where(c == 0, gt, ft), jnp.where(c == 0, ft, gt)

    def fellow(ft, gt):
        yt, zt = at(ft, gt)
        return 2 * (yt * RING + zt) + c

    def remote(src, dst, send, recv, dt, mt):
        return pltpu.make_async_remote_copy(
            src_ref=src,
            dst_ref=dst,
            send_sem=send,
            recv_sem=recv,
            device_id=(dt, mt),
            device_id_type=MESH,
        )

    def drain(ref, sem):
        pltpu.make_async_copy(ref, ref, sem).wait()

    def mate(k):
        return 2 * line + lax.div(k, 4), lax.rem(k, 4)

    loads = [
        pltpu.make_async_copy(hbm, ref, load.at[n])
        for n, (hbm, ref) in enumerate(
            ((act_hbm, act_ref), (td_hbm, td_ref), (q_hbm, q_ref), (kv_hbm, kv_ref))
        )
    ]
    for copy in loads:
        copy.start()
    results = [
        pltpu.make_async_copy(ref, hbm, keep.at[n])
        for n, (hbm, ref) in enumerate(
            (
                (down_hbm, down_ref),
                (scale_hbm, scale_ref),
                (moe_hbm, moe_ref),
                (ctx_hbm, ctx_ref),
            )
        )
    ]

    barrier = pltpu.get_barrier_semaphore()

    def greet(i, _):
        pl.semaphore_signal(
            barrier, inc=1, device_id=(lax.rem(d + i, 128), m), device_id_type=MESH
        )
        return 0

    lax.fori_loop(1, 128, greet, 0)
    for dx in range(1, 4):
        for cc in range(2):
            pl.semaphore_signal(
                barrier,
                inc=1,
                device_id=(2 * line + cc, lax.rem(m + dx, 4)),
                device_id_type=MESH,
            )

    def iota(shape, axis):
        return lax.broadcasted_iota(jnp.int32, shape, axis)

    def low3(v):
        return lax.bitwise_and(v, 7)

    def high3(v):
        return lax.shift_right_logical(v, 3)

    def column_of(v):
        return jnp.sum(jnp.where(iota((64, 64), 0) == iota((64, 64), 1), v, 0), axis=1, keepdims=True)

    spread = (low3(iota((8, 64), 1)) == iota((8, 64), 0)).astype(F32).astype(BF16)
    held = high3(iota((8, 64), 1)) == iota((8, 64), 0)

    def along(v):
        return jnp.where(held, jnp.dot(v.astype(BF16), spread, preferred_element_type=F32), 0.0)

    flat = jnp.sum(along(picks_ref[...].astype(F32)), axis=0, keepdims=True).astype(jnp.int32)
    owner = column_of(owner_ref[...])
    group = jnp.sum(jnp.where(iota((64, 64), 0) == flat, owner, 0), axis=0, keepdims=True)
    twin = (column_of(flat) == flat) & (iota((64, 64), 0) < iota((64, 64), 1))
    place = jnp.sum(twin.astype(jnp.int32), axis=0, keepdims=True)
    yg, zg = high3(group), low3(group)
    gates = jax.nn.sigmoid(logit_ref[...])
    shares = ROUTE_SCALE * (gates / jnp.sum(gates, axis=1, keepdims=True))
    coarse = shares.astype(BF16).astype(F32)
    coarse, fine = along(coarse).astype(BF16), along(shares - coarse).astype(BF16)
    for core, (gt, ft) in enumerate(((yg, zg), (zg, yg))):
        key = column_of(gt * 128 + ft * 16 + j * 2 + place)
        spots = (iota((64, 1024), 1) == key).astype(F32).astype(BF16)
        coef = jnp.dot(coarse, spots, preferred_element_type=F32)
        coef += jnp.dot(fine, spots, preferred_element_type=F32)
        for n in range(RING):
            coef_ref[core, n] = coef[:, n * 128 : (n + 1) * 128]
    kline[j] = coef_ref[c]

    row = low3(yg + zg + y + z) * 16 + yg * 2 + place
    chooser = (iota((128, 64), 0) == row).astype(F32).astype(BF16)
    loads[0].wait()
    acts = act_ref[...].astype(F32).reshape(64, HIDDEN).astype(BF16)
    packed = jnp.dot(chooser, acts, preferred_element_type=F32).astype(BF16)
    asend[...] = packed.reshape(RING, 16, HIDDEN)
    arecv[j] = asend[j]

    pl.semaphore_wait(barrier, 133)

    def a_copy(dj):
        jt = lax.rem(j + dj, RING)
        dt, mt = mate(jt)
        return remote(asend.at[jt], arecv.at[j], a_send.at[dj], a_recv.at[j], dt, mt)

    def a_arrival(dj):
        js = lax.rem(j + dj, RING)
        return remote(asend.at[js], arecv.at[js], a_send.at[dj], a_recv.at[js], d, m)

    for dj in range(1, RING):
        a_copy(dj).start()

    def k_copy(dj):
        jt = lax.rem(j + dj, RING)
        dt, mt = mate(jt)
        src = coef_ref.at[lax.div(jt, 4)]
        return remote(src, kline.at[j], k_send.at[dj], k_recv.at[j], dt, mt)

    for dj in range(1, RING):
        k_copy(dj).start()

    def columns(part):
        first, last = PARTS[part]
        return slice(first * 128, last * 128)

    def w_line(t):
        dy, dz = offset(lax.div(t, RING), lax.rem(t, RING))
        return mod8(y + dy) * RING + mod8(z + dz)

    def w_give(t, cc, part):
        cols = columns(part)
        return wsend.at[2 * t + cc, :, cols], wrecv.at[d, :, cols], w_recv.at[part, y]

    def w_send_line(t, part):
        lt = w_line(t)
        for cc in range(2):
            src, dst, sem = w_give(t, cc, part)
            remote(src, dst, w_send, sem, 2 * lt + cc, m).start()

    def w_step(t, _):
        blk = td_ref[src_ref[w_line(t)]]
        for cc in range(2):
            wsend[2 * t + cc] = blk[:, cc * WIDE : (cc + 1) * WIDE]
        w_send_line(t, 0)
        return 0

    def w_rest(t, _):
        w_send_line(t, 1)
        return 0

    def w_own(part):
        src, dst, sem = w_give(0, 1 - c, part)
        remote(src, dst, w_send, sem, 2 * line + 1 - c, m).start()
        src, dst, sem = w_give(0, c, part)
        pltpu.make_async_copy(src, dst, sem).start()

    loads[1].wait()
    own = td_ref[src_ref[line]]
    for cc in range(2):
        wsend[cc] = own[:, cc * WIDE : (cc + 1) * WIDE]
    w_own(0)
    lax.fori_loop(1, 18, w_step, 0)

    lax.fori_loop(18, 32, w_step, 0)

    for dj in range(1, RING):
        a_arrival(dj).wait_recv()
    ro = lax.broadcasted_iota(jnp.int32, (128, 128), 0)
    co = lax.broadcasted_iota(jnp.int32, (128, 128), 1)
    want = lax.bitwise_and(lax.shift_right_logical(ro, 1), 7) * 16
    want = want + lax.shift_right_logical(ro, 4) * 2 + lax.bitwise_and(ro, 1)
    perm = (co == want).astype(F32).astype(BF16)
    regrouped = jnp.dot(perm, arecv[...].reshape(128, HIDDEN), preferred_element_type=F32)
    bsend[...] = regrouped.astype(BF16).reshape(RING, 16, HIDDEN)
    r_out = lax.rem(y + z, RING)
    r_in = mod8(j - y - z)

    def b_target(dy):
        yg = mod8(y + dy)
        return yg, yg * RING + mod8(j - y - z - yg)

    def b_copy(dy):
        yg, gl = b_target(dy)
        return remote(
            bsend.at[yg], afull.at[r_out * RING + y], b_send.at[yg], b_recv, 2 * gl + c, m
        )

    for dy in range(RING):
        yg, gl = b_target(dy)

        @pl.when(gl != line)
        def _():
            b_copy(dy).start()

        @pl.when(gl == line)
        def _():
            pltpu.make_async_copy(bsend.at[yg], afull.at[r_out * RING + y], b_recv).start()

    for dj in range(1, RING):
        js = lax.rem(j + dj, RING)
        remote(kout, kline.at[js], k_send.at[dj], k_recv.at[js], d, m).wait_recv()
    kout[...] = sum(kline[n] for n in range(RING))
    kfin[g] = kout[g]

    def l_copy(dg):
        gt = mod8(g + dg)
        return remote(kout.at[gt], kfin.at[g], l_send.at[dg], l_recv.at[g], fellow(f, gt), m)

    for dg in range(1, RING):
        l_copy(dg).start()

    lax.fori_loop(32, 60, w_step, 0)

    mine = afull.at[pl.ds(r_in * RING, RING)]
    drain(mine, b_recv)

    def gathered(js):
        return mod8(js - y - z)

    def c_copy(dx, js):
        r = gathered(js)
        part = afull.at[pl.ds(r * RING, RING)]
        dt = 2 * line + (1 - c if dx == 0 else c)
        sem = c_send.at[dx] if js is j else c_send.at[4 + lax.rem(js - m + 4, 4)]
        return remote(part, part, sem, c_recv.at[r], dt, lax.rem(m + dx, 4))

    def along_x(dx):
        return c * 4 + lax.rem(m + dx, 4)

    for dx in range(4):
        c_copy(dx, j).start()

    lax.fori_loop(60, 64, w_step, 0)
    w_own(1)
    lax.fori_loop(1, 48, w_rest, 0)

    for dx in range(1, 4):
        js = along_x(dx)
        c_copy(0, js).wait_recv()
        c_copy(0, js).start()

    lax.fori_loop(48, 64, w_rest, 0)

    loads[2].wait()
    loads[3].wait()
    query = q_ref[0]
    cache = kv_ref[0]
    scores = (
        lax.dot_general(query, cache, (((0,), (0,)), ((), ())), preferred_element_type=F32)
        * SCORE_SCALE
    )
    span = scores.shape[1]
    live = (m * span + lax.broadcasted_iota(jnp.int32, scores.shape, 1)) < len_ref[0]
    masked = jnp.where(live, scores, -1e30)
    peak = jnp.max(masked, axis=1, keepdims=True)
    probs = jnp.where(live, jnp.exp(masked - peak), 0.0)
    total = jnp.sum(probs, axis=1, keepdims=True)
    mixed = lax.dot_general(
        probs.astype(BF16),
        cache[:LATENT],
        (((1,), (1,)), ((), ())),
        preferred_element_type=F32,
    )
    lane = lax.broadcasted_iota(jnp.int32, (128, 128), 1)
    xacc[m] = mixed.astype(BF16)
    xstat[m] = jnp.where(lane < 64, peak, total)

    def x_copies(dx):
        mt = lax.rem(m + dx, 4)
        return (
            remote(xacc.at[m], xacc.at[m], x_send.at[0, dx], x_recv.at[0, m], d, mt),
            remote(xstat.at[m], xstat.at[m], x_send.at[1, dx], x_recv.at[1, m], d, mt),
        )

    for dx in range(1, 4):
        for copy in x_copies(dx):
            copy.start()

    def quantize(part, i):
        ys = mod8(y - swing(lax.rem(i + RING - 1, RING)))
        rows = wrecv.at[pl.ds(16 * ys, 16), :, columns(part)]
        drain(rows, w_recv.at[part, ys])
        first, last = PARTS[part]
        w = rows[...].astype(F32).reshape(128, (last - first) * 128)
        row = jnp.zeros((1, 128), F32)
        for b in range(first, last):
            blk = w[:, (b - first) * 128 : (b - first + 1) * 128]
            top = jnp.max(jnp.max(jnp.abs(blk), axis=0, keepdims=True), axis=1, keepdims=True) + EPS
            scale = top / CODE_TOP
            coded = (blk * (CODE_TOP / top)).astype(BF16)
            down_ref[pl.ds(128 * ys, 128), b * 128 : (b + 1) * 128] = coded
            usable[pl.ds(128 * ys, 128), b * 128 : (b + 1) * 128] = (
                coded.astype(F32) * scale
            ).astype(BF16)
            row = jnp.where(iota((1, 128), 1) == b, scale, row)
        scl[part, pl.ds(ys, 1), :] = row

    def requantize(part):
        def step(i, _):
            quantize(part, i)
            return 0

        lax.fori_loop(0, RING, step, 0)

    requantize(0)

    for dx in range(4):
        js = (1 - c) * 4 + lax.rem(m + dx, 4)
        c_copy(0, js).wait_recv()

    def give(part, turn):
        ft = mod8(f + swing(lax.rem(turn + 1, RING)))
        cols = columns(part)
        return ft, psend.at[turn, :, cols], precv.at[f, :, cols], p_recv.at[part]

    def project(part):
        def step(turn, _):
            ft, src, dst, sem = give(part, turn)
            parts = []
            for dg in SIDE:
                yt, zt = at(ft, mod8(g + dg))
                parts.append(afull[mod8(yt + zt) * RING + yt])
            rows = jnp.concatenate(parts, axis=0)
            weights = usable[:, columns(part)]
            src[...] = jnp.dot(rows, weights, preferred_element_type=F32).astype(BF16)

            @pl.when(turn < RING - 1)
            def _():
                remote(src, dst, p_send, sem, fellow(ft, g), m).start()

            @pl.when(turn == RING - 1)
            def _():
                pltpu.make_async_copy(src, dst, sem).start()

            return 0

        lax.fori_loop(0, RING, step, 0)

    project(0)
    requantize(1)
    results[0].start()
    for b in range(BLOCKS):
        scale_ref[b] = jnp.sum(
            jnp.where(iota((8, 8), 0) == iota((8, 8), 1), scl[b // 5, :, b : b + 1], 0.0),
            axis=0,
            keepdims=True,
        )
    results[1].start()

    project(1)

    for dx in range(1, 4):
        ms = lax.rem(m + dx, 4)
        remote(xacc.at[ms], xacc.at[ms], x_send.at[0, dx], x_recv.at[0, ms], d, m).wait_recv()
        remote(xstat.at[ms], xstat.at[ms], x_send.at[1, dx], x_recv.at[1, ms], d, m).wait_recv()
    peaks = [xstat[s][:, 0:1] for s in range(4)]
    highest = jnp.maximum(jnp.maximum(peaks[0], peaks[1]), jnp.maximum(peaks[2], peaks[3]))
    weight = jnp.zeros((128, 1), F32)
    blend = jnp.zeros((128, LATENT), F32)
    for s in range(4):
        factor = jnp.exp(peaks[s] - highest)
        weight = weight + xstat[s][:, 64:65] * factor
        blend = blend + xacc[s].astype(F32) * factor
    ctx_ref[...] = (blend / weight).astype(BF16)
    results[3].start()

    for dg in range(1, RING):
        gs = mod8(g + dg)
        remote(kout.at[gs], kfin.at[gs], l_send.at[dg], l_recv.at[gs], d, m).wait_recv()
    mates = high3(iota((64, 128), 0)) == low3(lax.shift_right_logical(iota((64, 128), 1), 1))
    for part in range(2):
        cols = columns(part)
        drain(precv.at[:, :, cols], p_recv.at[part])
        for b in range(RING):
            gt = mod8(g + SIDE[b])
            share = jnp.where(mates, jnp.concatenate([kfin[gt]] * RING, axis=0), 0.0)
            high = share.astype(BF16)
            low = (share - high.astype(F32)).astype(BF16)
            got = precv[:, 16 * b : 16 * b + 16, cols].reshape(128, cols.stop - cols.start)
            both = jnp.dot(jnp.concatenate([high, low], axis=0), got, preferred_element_type=F32)
            src, dst = qsend.at[b, :, cols], qrecv.at[b, :, cols]
            src[...] = (both[:64] + both[64:]).astype(BF16)
            if SIDE[b]:
                remote(src, dst, q_send, q_recv.at[part], fellow(f, gt), m).start()
            else:
                pltpu.make_async_copy(src, dst, q_recv.at[part]).start()

    for part in range(2):
        cols = columns(part)
        drain(qrecv.at[:, :, cols], q_recv.at[part])
        full = qrecv[0, :, cols].astype(F32)
        for b in range(1, RING):
            full = full + qrecv[b, :, cols].astype(F32)
        moesend[:, :, cols] = full.reshape(RING, 8, cols.stop - cols.start).astype(BF16)

    def m_copy(dj):
        jt = lax.rem(j + dj, RING)
        dt, mt = mate(jt)
        return remote(moesend.at[jt], moerecv.at[j], m_send.at[dj], m_recv.at[j], dt, mt)

    for dj in range(1, RING):
        m_copy(dj).start()
    moerecv[j] = moesend[j]
    for dj in range(1, RING):
        js = lax.rem(j + dj, RING)
        remote(moesend.at[js], moerecv.at[js], m_send.at[dj], m_recv.at[js], d, m).wait_recv()
    for mm in range(4):
        for cc in range(2):
            start = (2 * mm + cc) * WIDE
            moe_ref[:, start : start + WIDE] = moerecv[cc * 4 + mm]
    results[2].start()

    for dj in range(1, RING):
        a_copy(dj).wait_send()
        k_copy(dj).wait_send()
        l_copy(dj).wait_send()
        m_copy(dj).wait_send()
    for dx in range(4):
        c_copy(dx, j).wait_send()
    for dx in range(1, 4):
        c_copy(0, along_x(dx)).wait_send()
        for copy in x_copies(dx):
            copy.wait_send()
    for dy in range(RING):
        yg, gl = b_target(dy)

        @pl.when(gl != line)
        def _():
            b_copy(dy).wait_send()

    drain(wsend.at[pl.ds(0, 127)], w_send)
    drain(psend.at[pl.ds(0, 7)], p_send)
    drain(qsend.at[pl.ds(0, 7)], q_send)
    for copy in results:
        copy.wait()


def hand_out(*refs):
    given, out, held, sem = refs[:4], refs[4:8], refs[8:12], refs[12]
    quarter = HIDDEN // 4
    pieces = [(0, pl.ds(n * quarter, quarter)) for n in range(4)] + [(1, None), (2, None), (3, None)]

    def copy(src, dst, n):
        which, rows = pieces[n]
        if rows is None:
            return pltpu.make_async_copy(src[which], dst[which], sem.at[n])
        return pltpu.make_async_copy(src[which].at[rows], dst[which].at[rows], sem.at[n])

    for n in range(7):
        copy(given, held, n).start()
    for n in range(7):
        copy(given, held, n).wait()
        copy(held, out, n).start()
    for n in range(7):
        copy(held, out, n).wait()


def per_device(
    train_down, owner, trainer_slot, expert_act, picks, route_logits, queries, kv_cache, lengths
):
    groups = jnp.arange(64, dtype=jnp.int32)
    source = jnp.sum(jnp.where(owner[None, :] == groups[:, None], trainer_slot[None, :], 0), axis=1)
    vmem = pl.BlockSpec(memory_space=pltpu.VMEM)
    smem = pl.BlockSpec(memory_space=pltpu.SMEM)
    dma = pltpu.SemaphoreType.DMA
    hbm = pl.BlockSpec(memory_space=pltpu.HBM)
    out_shape = (
        jax.ShapeDtypeStruct((HIDDEN, WIDE), BF16),
        jax.ShapeDtypeStruct((BLOCKS, 1, RING), F32),
        jax.ShapeDtypeStruct((8, 8 * WIDE), BF16),
        jax.ShapeDtypeStruct((128, LATENT), BF16),
    )
    found = pl.pallas_call(
        kernel,
        out_shape=out_shape,
        in_specs=[smem, smem] + [vmem] * 3 + [hbm] * 4,
        out_specs=(pl.BlockSpec(memory_space=pl.ANY),) * 4,
        scratch_shapes=[pltpu.VMEM(out.shape, out.dtype) for out in out_shape]
        + [
            pltpu.VMEM(train_down.shape, BF16),
            pltpu.VMEM(expert_act.shape, BF16),
            pltpu.VMEM((1, 576, 128), BF16),
            pltpu.VMEM((1, 576, 512), BF16),
            pltpu.VMEM((2, RING, 8, 128), F32),
            pltpu.VMEM((128, 8, WIDE), BF16),
            pltpu.VMEM((128, 8, WIDE), BF16),
            pltpu.VMEM((RING, 16, HIDDEN), BF16),
            pltpu.VMEM((RING, 16, HIDDEN), BF16),
            pltpu.VMEM((RING, 16, HIDDEN), BF16),
            pltpu.VMEM((64, 16, HIDDEN), BF16),
            pltpu.VMEM((HIDDEN, WIDE), BF16),
            pltpu.VMEM((RING, 128, WIDE), BF16),
            pltpu.VMEM((RING, 128, WIDE), BF16),
            pltpu.VMEM((RING, 64, WIDE), BF16),
            pltpu.VMEM((RING, 64, WIDE), BF16),
            pltpu.VMEM((RING, RING, 8, 128), F32),
            pltpu.VMEM((RING, 8, 128), F32),
            pltpu.VMEM((RING, 8, 128), F32),
            pltpu.VMEM((4, 128, LATENT), BF16),
            pltpu.VMEM((4, 128, 128), F32),
            pltpu.VMEM((RING, 8, WIDE), BF16),
            pltpu.VMEM((RING, 8, WIDE), BF16),
            pltpu.VMEM((2, RING, 128), F32),
            dma((4,)),
            dma((4,)),
            dma((RING,)),
            dma((RING,)),
            dma((RING,)),
            dma,
            dma((RING,)),
            dma((RING,)),
            dma((RING,)),
            dma((RING,)),
            dma((RING,)),
            dma((RING,)),
            dma,
            dma((2, RING)),
            dma,
            dma((2,)),
            dma,
            dma((2,)),
            dma((2, 4)),
            dma((2, 4)),
            dma((RING,)),
            dma((RING,)),
        ],
        compiler_params=pltpu.CompilerParams(
            collective_id=0, has_side_effects=True, vmem_limit_bytes=LIMIT
        ),
        cost_estimate=pl.CostEstimate(
            flops=2_200_000_000, bytes_accessed=8_000_000, transcendentals=70_000
        ),
    )(
        source,
        lengths,
        owner.reshape(1, 64),
        picks,
        route_logits,
        train_down,
        expert_act,
        queries.transpose(0, 2, 1),
        kv_cache.transpose(0, 2, 1),
    )
    anywhere = pl.BlockSpec(memory_space=pl.ANY)
    down, scale, moe, context = pl.pallas_call(
        hand_out,
        out_shape=out_shape,
        in_specs=[anywhere] * 4,
        out_specs=(anywhere,) * 4,
        scratch_shapes=[pltpu.VMEM(out.shape, out.dtype) for out in out_shape] + [dma((7,))],
        compiler_params=pltpu.CompilerParams(vmem_limit_bytes=LIMIT),
    )(*found)
    return (
        down.reshape(1, HIDDEN, WIDE),
        scale.transpose(1, 2, 0),
        moe,
        context.reshape(1, 128, LATENT),
    )


def solution(mesh):
    placed = (
        P(None, "dp", "mp"),
        P(),
        P(),
        P(("dp", "mp"), None, None),
        P(("dp", "mp"), None),
        P(("dp", "mp"), None),
        P("dp", None, None),
        P("dp", "mp", None),
        P("dp"),
    )
    return jax.shard_map(
        per_device,
        mesh=mesh,
        in_specs=placed,
        out_specs=(
            P("dp", None, "mp"),
            P("dp", None, "mp"),
            P(("dp", "mp"), None),
            P("dp", None, None),
        ),
        check_vma=False,
    )
```
